512 devices in a mesh: group: 64 (over z, x), pair: 8 (over y, core).
Axes of the slice: x: 4, y: 4, z: 16, core: 2. Of those that a mesh axis runs over, the one named last changes fastest.
Arguments:
- embeddings: bfloat16 [32768, 4096], P(('group', 'pair')), may hold values from -6 to 6
- dest: int32 [32768, 1], replicated, may hold values from 0 to 63; in each aligned block of 64 rows (0 to 63, 64 to 127, ...) at most 2 rows name the same one
- labels: int32 [64, 8], P('group'), may hold values from 0 to 4, never falling along the last dimension, each value on 1 to 2 neighbouring positions
Outputs:
- smoothed: bfloat16 [32768, 4096], P(('group', 'pair'))
The draws below stay inside these ranges and needn't reach their ends.
Inputs may be any that keep to these rules, and one draw needn't show every extreme that they name: `dest`: in each aligned block of 64 rows (one source cell) at most 2 documents name one owner group, and exactly 2 for some. `labels`: each row is non-falling along pair, with 5 clusters of one or two consecutive blocks.
All inputs are finite; a program needn't handle non-finite values.
Results may differ from the reference program's by a relative error of at most 0.0075.
Values may be sent and summed in bfloat16 or wider, within the bound.
A program may use at most 64 MiB of HBM per device.

```python
import math
import jax
import jax.numpy as jnp
import numpy as np
from jax import lax

D = 4096
DOC_DEV = 64
CAP = 2
DOCS = 32768
CLUSTERS = 5
N_GROUP = 64
N_PAIR = 8


def block_scale(stream_key, dims, pieces, smallest, high):
    gain, own = 1.0, jax.random.fold_in(stream_key, 6)
    for axis_at, shards_of in pieces:
        heights = jnp.exp(jax.random.uniform(jax.random.fold_in(own, axis_at), (shards_of,), jnp.float32, smallest / len(pieces), high / len(pieces)))
        gain = gain * jnp.repeat(heights, dims[axis_at] // shards_of).reshape([-1 if axis == axis_at else 1 for axis in range(len(dims))])
    return gain


def profile(amount, total, bound, lean):
    loads = [(1 << 20) // math.isqrt(standing ** lean) + 1 for standing in range(2, amount + 1)]
    spare, counts = total - bound - (amount - 1), [1] * (amount - 1)
    while spare > 0:
        movable = [i for i in range(amount - 1) if counts[i] < bound]
        pool, budget = sum([loads[i] for i in movable]), spare
        for i in movable:
            addition = min(bound - counts[i], max(1, budget * loads[i] // pool), spare)
            counts[i] = counts[i] + addition
            spare = spare - addition
    return np.array([bound] + counts)


def ragged_sizes(key, count, total, most, skew):
    if count == 2:
        one = jax.random.randint(key, (), max(1, total - most), min(most, total - 1) + 1)
        return jnp.stack([one, total - one])
    lengths = jnp.asarray(profile(count, total, most, skew), jnp.int32)
    pairs = (count - 1) // 2
    giver, taker = lengths[1:1 + 2 * pairs:2], lengths[2:2 + 2 * pairs:2]
    slack = jnp.minimum(giver - 1, most - taker)
    passed = jax.random.randint(jax.random.fold_in(key, 1), (pairs,), 0, 1 << 20) % (slack + 1)
    lengths = lengths.at[1:1 + 2 * pairs:2].set(giver - passed).at[2:2 + 2 * pairs:2].set(taker + passed)
    return lengths[jax.random.permutation(jax.random.fold_in(key, 2), count)]


def routed_block(own_key, own, number, rows, count, top, bound, skew):
    ranking = jax.random.permutation(own_key, count)
    packed, common = portions_of(count, rows * top, bound, skew, True), portions_of(count, rows * top, bound, skew, False)
    places = jnp.arange(count)

    def named(lengths, turn):
        used = int((lengths > 0).sum())
        fixed = max(1, used // 4)
        passed = fixed + (places - fixed + turn * (used - fixed)) % max(1, count - fixed)
        return jnp.zeros((count,), jnp.int32).at[ranking[jnp.where(places < fixed, places, passed)]].set(jnp.asarray(lengths, jnp.int32))

    lengths = jnp.where(number % 4 == 0, named(packed, number // 4), named(common, number - number // 4 - 1))
    mixed = jax.random.permutation(jax.random.fold_in(own, 3), count)
    donor, sink = mixed[0:count // 2 * 2:2], mixed[1:count // 2 * 2:2]
    room = jnp.minimum(lengths[donor] - 1, bound - lengths[sink]) // 2
    room = jnp.where((donor == ranking[0]) | (sink == ranking[0]) | (lengths[sink] == 0), 0, jnp.maximum(room, 0))
    passed = jax.random.randint(jax.random.fold_in(own, 4), (count // 2,), 0, 1 << 20) % (room + 1)
    lengths = lengths.at[donor].add(-passed).at[sink].add(passed)
    items = jnp.searchsorted(jnp.cumsum(lengths), jnp.arange(rows * top), side="right").astype(jnp.int32)
    grid = items.reshape(top, rows).T
    grid = grid[jax.random.permutation(jax.random.fold_in(own, 1), rows)]
    turn = jax.random.randint(jax.random.fold_in(own, 2), (rows, 1), 0, top)
    return jnp.take_along_axis(grid, (jnp.arange(top)[None, :] + turn) % top, axis=1)


def portions_of(amount, total, reach, lean, full):
    weights = [(1 << 20) // math.isqrt(grade ** lean) + 1 for grade in range(1, amount + 1)]
    largest = reach if full else min(reach, max(-(-total // amount), total * weights[0] // sum(weights)))
    least = 1 if total - largest >= amount - 1 else 0
    holding, rest = [largest] + [least] * (amount - 1), total - largest - least * (amount - 1)
    while rest > 0:
        free = [i for i in range(1, amount) if holding[i] < largest] or [i for i in range(1, amount) if holding[i] < reach]
        mass, remaining = sum([weights[i] for i in free]), rest
        for i in free:
            extra = min(reach - holding[i], max(1, remaining * weights[i] // mass), rest)
            holding[i] = holding[i] + extra
            rest = rest - extra
    return np.array(holding)


def scatter_about(rng, dims, scale, limit, split=(), kind=jnp.bfloat16):
    values = scale * jax.random.normal(rng, dims, jnp.float32)
    if split:
        values = values * block_scale(rng, dims, split, -0.22, 0.18)
    return jnp.clip(values, -limit, limit).astype(kind)


def setup_inputs(seed: int = 0) -> dict:
    keys = jax.random.split(jax.random.key(seed), 4)
    embeddings = scatter_about(keys[0], (DOCS, D), 1.0, 6.0, ((0, 512),))
    dest_keys = jax.random.split(jax.random.fold_in(keys[1], 1), DOCS // DOC_DEV)
    dest_turns = jax.random.permutation(jax.random.fold_in(keys[1], 3), DOCS // DOC_DEV)
    dest = jax.vmap(lambda own, number: routed_block(jax.random.fold_in(keys[1], 2), own, number, DOC_DEV, N_GROUP, 1, CAP, 2))(dest_keys, dest_turns).reshape((DOCS, 1))
    labels = jax.vmap(lambda own: jnp.searchsorted(jnp.cumsum(ragged_sizes(own, CLUSTERS, N_PAIR, 2, 0)), jnp.arange(N_PAIR), side="right"))(jax.random.split(keys[2], N_GROUP)).reshape((N_GROUP, N_PAIR)).astype(jnp.int32)
    return {"embeddings": embeddings, "dest": dest, "labels": labels}


score_scale = 64.0
self_weight = math.exp(4.0)

def normalized(rows):
    values = rows.astype(jnp.float32)
    factor = lax.rsqrt(lax.optimization_barrier(jnp.mean(values * values, axis=-1, keepdims=True)) + 1e-05)
    return (values * factor * (1.0 / math.sqrt(values.shape[-1]))).astype(jnp.bfloat16)

def slot_numbers(routes, groups, capacity):
    hits = (routes[..., None] == jnp.arange(groups, dtype=jnp.int32)).astype(jnp.int32)
    ranks = lax.optimization_barrier(jnp.sum(jnp.cumsum(hits, axis=-2) * hits, axis=-1)) - 1
    return routes * capacity + ranks

def rounded(weights):
    return lax.optimization_barrier(weights.astype(jnp.bfloat16)).astype(jnp.float32)

def smooth_group(items):
    blocks, live, marks = items
    pairs, slots, width = blocks.shape
    wide = blocks.astype(jnp.float32)
    apart = 1.0 - jnp.eye(slots, dtype=jnp.float32)
    diag = jnp.exp(score_scale * jnp.einsum('qid,qjd->qij', wide, wide)) * live[:, None, :] * apart
    joined = (marks[:-1] == marks[1:]).astype(jnp.float32)
    off = jnp.exp(score_scale * jnp.einsum('qid,qjd->qij', wide[:-1], wide[1:]))
    off = off * live[:-1, :, None] * live[1:, None, :] * joined[:, None, None]
    diag_r = rounded(diag)
    off_r = rounded(off)
    rows_part = jnp.einsum('qij,qjd->qid', off_r, wide[1:])
    cols_part = jnp.einsum('qij,qid->qjd', off_r, wide[:-1])
    empty = jnp.zeros((1, slots, width), jnp.float32)
    numer = self_weight * wide + jnp.einsum('qij,qjd->qid', diag_r, wide)
    numer = numer + jnp.concatenate([rows_part, empty], axis=0) + jnp.concatenate([empty, cols_part], axis=0)
    flat = jnp.zeros((1, slots), jnp.float32)
    denom = self_weight + lax.optimization_barrier(jnp.sum(diag, axis=-1))
    denom = denom + jnp.concatenate([lax.optimization_barrier(jnp.sum(off, axis=2)), flat], axis=0) + jnp.concatenate([flat, lax.optimization_barrier(jnp.sum(off, axis=1))], axis=0)
    return (math.sqrt(width) * numer / denom[..., None]).astype(jnp.bfloat16)

def pick_rows(table, index):
    return jax.vmap(jax.vmap(lambda rows, where: rows[where]))(table, index)

def reference(embeddings, dest, labels):
    groups = N_GROUP
    pairs = N_PAIR
    count = DOC_DEV
    slots = groups * CAP
    width = embeddings.shape[1]
    routes = dest.reshape(groups, pairs, count)
    slot = slot_numbers(routes, groups, CAP)
    hat = normalized(embeddings).reshape(groups, pairs, count, width)
    match = (slot[:, :, None, :] == jnp.arange(slots, dtype=jnp.int32)[:, None]).astype(jnp.int32)
    slot_doc = lax.optimization_barrier(jnp.sum(match * jnp.arange(count, dtype=jnp.int32), axis=-1)).astype(jnp.int32)
    filled = lax.optimization_barrier(jnp.sum(match, axis=-1))
    outgoing = pick_rows(hat, slot_doc)
    outgoing = jnp.where(filled[..., None] > 0, outgoing, jnp.zeros((), jnp.bfloat16))
    blocks = outgoing.reshape(groups, pairs, groups, CAP, width).transpose(2, 1, 0, 3, 4).reshape(groups, pairs, slots, width)
    live = filled.reshape(groups, pairs, groups, CAP).transpose(2, 1, 0, 3).reshape(groups, pairs, slots).astype(jnp.float32)
    block_out = lax.map(smooth_group, (blocks, live, labels))
    back = block_out.reshape(groups, pairs, groups, CAP, width).transpose(2, 1, 0, 3, 4).reshape(groups, pairs, slots, width)
    result = pick_rows(back, slot)
    return result.reshape(groups * pairs * count, width)
```

```python
import math

import jax
import jax.numpy as jnp
from jax import lax
from jax.experimental import pallas as pl
from jax.experimental.pallas import tpu as pltpu
from jax.sharding import PartitionSpec as P

score_scale = 64.0
self_weight = math.exp(4.0)
along_rows = (((1,), (1,)), ((), ()))
along_cols = (((0,), (0,)), ((), ()))


def shifted(block, axis, distance):
    devices = range(lax.axis_size(axis))
    route = [(i - distance, i) for i in devices if i - distance in devices]
    return lax.ppermute(block, axis, route)


def normalized(rows):
    values = rows.astype(jnp.float32)
    factor = lax.rsqrt(jnp.mean(values * values, axis=-1, keepdims=True) + 1e-05)
    return (values * factor * (1.0 / math.sqrt(values.shape[-1]))).astype(jnp.bfloat16)


def live_slots(routes, source_pair, owner, capacity):
    column = lax.dynamic_index_in_dim(routes, source_pair, axis=1, keepdims=False)
    counts = jnp.sum((column == owner).astype(jnp.int32), axis=1)
    return (
        (jnp.arange(capacity, dtype=jnp.int32)[None, :] < counts[:, None])
        .reshape(-1)
        .astype(jnp.float32)
    )


def pair_weights(left, right, mask):
    scores = lax.dot_general(left, right, along_rows, preferred_element_type=jnp.float32)
    return jnp.exp(score_scale * scores) * mask


def padded(embeddings, dest, labels):
    groups = lax.axis_size("group")
    pairs = lax.axis_size("pair")
    group_at = lax.axis_index("group")
    pair_at = lax.axis_index("pair")
    count = embeddings.shape[0]
    width = embeddings.shape[1]
    capacity = 2 * count // groups
    slots = groups * capacity
    routes = dest.reshape(groups, pairs, count)
    own_routes = lax.dynamic_index_in_dim(
        lax.dynamic_index_in_dim(routes, group_at, axis=0, keepdims=False),
        pair_at,
        axis=0,
        keepdims=False,
    )
    hits = (own_routes[:, None] == jnp.arange(groups, dtype=jnp.int32)[None, :]).astype(jnp.int32)
    ranks = jnp.sum(jnp.cumsum(hits, axis=0) * hits, axis=1) - 1
    slot = own_routes * capacity + ranks
    match = (slot[None, :] == jnp.arange(slots, dtype=jnp.int32)[:, None]).astype(jnp.int32)
    slot_doc = jnp.sum(match * jnp.arange(count, dtype=jnp.int32)[None, :], axis=1)
    filled = jnp.sum(match, axis=1)
    hat = normalized(embeddings)
    outgoing = jnp.where(filled[:, None] > 0, hat[slot_doc], jnp.zeros((), jnp.bfloat16))
    arrived = lax.all_to_all(
        outgoing.reshape(groups, capacity, width), "group", split_axis=0, concat_axis=0, tiled=True
    )
    block = arrived.reshape(slots, width)
    marks = labels[0]
    mine = marks[pair_at]
    live_mine = live_slots(routes, pair_at, group_at, capacity)
    next_at = jnp.minimum(pair_at + 1, pairs - 1)
    joined_next = jnp.logical_and(pair_at + 1 < pairs, marks[next_at] == mine).astype(jnp.float32)
    live_next = live_slots(routes, next_at, group_at, capacity)
    apart = (jnp.arange(slots)[:, None] != jnp.arange(slots)[None, :]).astype(jnp.float32)
    own_weights = pair_weights(block, block, live_mine[None, :] * apart)
    numer = self_weight * block.astype(jnp.float32) + jnp.dot(
        own_weights.astype(jnp.bfloat16), block, preferred_element_type=jnp.float32
    )
    denom = self_weight + jnp.sum(own_weights, axis=1)
    neighbour = shifted(block, "pair", -1)
    next_weights = pair_weights(
        block, neighbour, live_mine[:, None] * live_next[None, :] * joined_next
    )
    next_rounded = next_weights.astype(jnp.bfloat16)
    numer = numer + jnp.dot(next_rounded, neighbour, preferred_element_type=jnp.float32)
    denom = denom + jnp.sum(next_weights, axis=1)
    column_numer = lax.dot_general(
        next_rounded, block, along_cols, preferred_element_type=jnp.float32
    )
    column_denom = jnp.sum(next_weights, axis=0)
    came_numer, came_denom = (
        shifted(column_numer.astype(jnp.bfloat16), "pair", 1).astype(column_numer.dtype),
        shifted(column_denom.astype(jnp.bfloat16), "pair", 1).astype(column_denom.dtype),
    )
    numer = numer + came_numer
    denom = denom + came_denom
    block_out = (math.sqrt(width) * numer / denom[:, None]).astype(jnp.bfloat16)
    returned = lax.all_to_all(
        block_out.reshape(groups, capacity, width), "group", split_axis=0, concat_axis=0, tiled=True
    )
    return returned.reshape(slots, width)[slot]


ZS, XS, PAIRS, COUNT, WIDTH = 16, 4, 8, 64, 4096
GROUPS = ZS * XS
SLOTS = XS + 1
SUB, LANE = 16, 256
BLOCK = GROUPS * 2
SENT = ZS * SLOTS
BATCH = 2
BATCHES = ZS // BATCH
MESH = pl.DeviceIdType.MESH
f32, bf16, i32 = jnp.float32, jnp.bfloat16, jnp.int32


def distance_at(t):
    half = t // 2
    far = jnp.where(t % 2 == 0, 8 - half, 8 + half)
    return jnp.where(t == 0, 0, far)


def step_of(distance):
    near = jnp.where(distance < 8, 16 - 2 * distance, 2 * distance - 15)
    return jnp.where(distance == 0, 0, near)


def mirror(t):
    return jnp.where(t < 2, t, jnp.where(t % 2 == 0, t + 1, t - 1))


def iota(shape, axis):
    return lax.broadcasted_iota(i32, shape, axis)


def compact_kernel(
    x_ref, dest_ref, lab_ref, out_ref, ok_ref,
    hat, wide, zsend, zland, own, beside, rows, outd, zback, cand, zret,
    mark, marks, counts, place, pick, unpick, sides, lives, choice, weights,
    lab_x_send, lab_x_recv, lab_z_send, lab_z_recv, z_send, z_recv, x_send, x_recv, y_send, y_recv,
    xb_send, xb_recv, zb_send, zb_recv,
):
    group = lax.axis_index("group")
    pair = lax.axis_index("pair")
    z, x = group // XS, group % XS

    def at(zz, xx):
        return (zz * XS + xx, pair)

    def z_peer(t):
        return lax.rem(z + distance_at(t), ZS)

    def x_peer(j):
        return lax.rem(x + j, XS)

    def pair_peer(side):
        return lax.rem(pair + jnp.where(side == 0, 1, PAIRS - 1), PAIRS)

    barrier = pltpu.get_barrier_semaphore()
    for d in range(1, ZS):
        pl.semaphore_signal(barrier, inc=1, device_id=at(lax.rem(z + d, ZS), x), device_id_type=MESH)
    for j in range(1, XS):
        pl.semaphore_signal(barrier, inc=1, device_id=at(z, x_peer(j)), device_id_type=MESH)
    for step in (1, PAIRS - 1):
        pl.semaphore_signal(
            barrier, inc=1, device_id=(group, lax.rem(pair + step, PAIRS)), device_id_type=MESH
        )

    @pl.loop(0, COUNT // 16)
    def _(i):
        r = pl.ds(pl.multiple_of(i * 16, 16), 16)
        values = x_ref[r, :].astype(f32)
        factor = lax.rsqrt(jnp.mean(values * values, axis=-1, keepdims=True) + 1e-05)
        hat[r, :] = (values * factor * (1.0 / math.sqrt(WIDTH))).astype(bf16)

    turned = dest_ref[...].T
    for parity in range(2):
        part = turned[parity * COUNT : (parity + 1) * COUNT, :]
        unit = jnp.left_shift(jnp.ones_like(part), (part & 7) * 4)
        for k in range(GROUPS // 8):
            held = jnp.sum(jnp.where((part >> 3) == k, unit, 0), axis=0, keepdims=True)
            nibble = jnp.broadcast_to(held, (8, 256)) >> (iota((8, 256), 0) * 4)
            counts[parity, 8 * k : 8 * k + 8, :] = (nibble & 3).astype(f32)
    second = [(counts[parity] == 2.0).astype(f32) for parity in range(2)]
    both = (second[0] + second[1]).astype(bf16)
    need_col = jnp.sum(second[0] + second[1], axis=1, keepdims=True)
    need_row = lax.dot_general(
        jnp.ones((8, 256), bf16), both, along_rows, preferred_element_type=f32
    )[0:1, :]
    g_col, g_row = iota((GROUPS, GROUPS), 0), iota((GROUPS, GROUPS), 1)
    ahead = jnp.logical_or(
        need_row > need_col, jnp.logical_and(need_row == need_col, g_row < g_col)
    )
    standing = jnp.sum(ahead.astype(i32), axis=1, keepdims=True)
    position = (standing % ZS) * XS + standing // ZS
    place[...] = jnp.broadcast_to(position, (GROUPS, 128))

    cell = group * (PAIRS // 2) + pair // 2
    line = dest_ref[pl.ds(cell, 1), :]
    lane = iota((1, 128), 1)
    mine = lane // COUNT == pair % 2
    line = jnp.where(mine, line, -1)
    eye = iota((128, 128), 0) == iota((128, 128), 1)
    line_col = jnp.sum(jnp.where(eye, jnp.broadcast_to(line, (128, 128)), 0), axis=1, keepdims=True)
    earlier = jnp.logical_and(line_col == line, iota((128, 128), 0) < iota((128, 128), 1))
    rank = jnp.sum(earlier.astype(i32), axis=0, keepdims=True)
    spot = jnp.sum(
        jnp.where(iota((GROUPS, 128), 0) == line, place[...], 0), axis=0, keepdims=True
    )
    step = step_of((spot // XS - z + ZS) % ZS)
    slot = step * SLOTS + jnp.where(rank == 0, spot % XS, XS)
    slot = jnp.where(mine, slot, -1)
    fold = slot[:, :COUNT] + slot[:, COUNT:] + 1
    slot_col = jnp.sum(
        jnp.where(
            iota((COUNT, COUNT), 0) == iota((COUNT, COUNT), 1),
            jnp.broadcast_to(fold, (COUNT, COUNT)),
            0,
        ),
        axis=1,
        keepdims=True,
    )
    pick[...] = (iota((SENT, COUNT), 0) == fold).astype(f32).astype(bf16)
    unpick[...] = (iota((COUNT, SENT), 1) == slot_col).astype(f32).astype(bf16)

    @pl.loop(0, SUB)
    def _(c):
        got = jnp.dot(
            pick[...],
            hat[:, pl.ds(pl.multiple_of(c * LANE, LANE), LANE)],
            preferred_element_type=f32,
        )
        spread(wide, c, SENT, got)

    mark[...] = jnp.zeros((1, 128), i32)
    mark[:, 0:PAIRS] = lab_ref[...]
    marks[pl.ds(group, 1), :, :] = mark[...].reshape(1, 1, 128)
    zland[0] = docs_of(wide, 0, SLOTS)

    pl.semaphore_wait(barrier, ZS - 1 + XS - 1 + 2)

    def lab_x(j):
        here = marks.at[pl.ds(group, 1)]
        return pltpu.make_async_remote_copy(
            here, here, lab_x_send.at[j], lab_x_recv.at[j],
            device_id=at(z, x_peer(j)), device_id_type=MESH,
        )

    def lab_z(t):
        here = marks.at[pl.ds(z * XS, XS)]
        return pltpu.make_async_remote_copy(
            here, here, lab_z_send.at[t], lab_z_recv.at[mirror(t)],
            device_id=at(z_peer(t), x), device_id_type=MESH,
        )

    def lab_z_arrival(t):
        there = marks.at[pl.ds(z_peer(t) * XS, XS)]
        return pltpu.make_async_remote_copy(
            there, there, lab_z_send.at[t], lab_z_recv.at[t],
            device_id=at(z_peer(t), x), device_id_type=MESH,
        )

    def lab_x_arrival(j):
        there = marks.at[pl.ds(z * XS + lax.rem(x + XS - j, XS), 1)]
        return pltpu.make_async_remote_copy(
            there, there, lab_x_send.at[j], lab_x_recv.at[j],
            device_id=at(z, x_peer(j)), device_id_type=MESH,
        )

    def z_out(t):
        return pltpu.make_async_remote_copy(
            zsend.at[t], zland.at[mirror(t)], z_send.at[t], z_recv.at[mirror(t)],
            device_id=at(z_peer(t), x), device_id_type=MESH,
        )

    def z_in(t):
        return pltpu.make_async_remote_copy(
            zsend.at[t], zland.at[t], z_send.at[t], z_recv.at[t],
            device_id=at(z_peer(t), x), device_id_type=MESH,
        )

    for j in range(1, XS):
        lab_x(j).start()

    @pl.loop(1, ZS)
    def _(t):
        zsend[t] = docs_of(wide, t * SLOTS, SLOTS)
        z_out(t).start()

    for j in range(1, XS):
        lab_x_arrival(j).wait_recv()

    @pl.loop(1, ZS)
    def _(t):
        lab_z(t).start()

    here = place[:, 0:1] == group
    held = [
        jnp.sum(jnp.where(here, counts[parity], 0.0), axis=0, keepdims=True) for parity in range(2)
    ]
    s_lane = iota((256, BLOCK), 1)
    s_source = lax.rem(z + distance_at(s_lane // (2 * XS)), ZS) * XS + (s_lane // 2) % XS
    for n, shift in enumerate((0, PAIRS - 1, 1)):
        other = lax.rem(pair + shift, PAIRS)
        row = jnp.where(other % 2 == 0, held[0], held[1])
        chosen = (iota((256, BLOCK), 0) == s_source * (PAIRS // 2) + other // 2).astype(f32)
        filled = jnp.dot(
            jnp.broadcast_to(row, (8, 256)).astype(bf16), chosen.astype(bf16),
            preferred_element_type=f32,
        )
        lives[n] = (filled > (iota((8, BLOCK), 1) % 2).astype(f32)).astype(f32)

    at_here = (place[:, 0:GROUPS] == z * XS + iota((GROUPS, GROUPS), 1) % XS).astype(f32)
    wanted = jnp.where(
        pair % 2 == 0, (counts[0] == 2.0).astype(f32), (counts[1] == 2.0).astype(f32)
    )
    owner_of = lax.dot_general(
        at_here.astype(bf16), wanted.astype(bf16), along_cols, preferred_element_type=f32
    )
    t_row = iota((GROUPS, 256), 0) // XS
    c_row = (lax.rem(z + distance_at(t_row), ZS) * XS + x) * (PAIRS // 2) + pair // 2
    choice[...] = jnp.broadcast_to(
        jnp.sum(jnp.where(iota((GROUPS, 256), 1) == c_row, owner_of, 0.0), axis=1, keepdims=True),
        (GROUPS, 128),
    )

    plane = (place[:, 0:ZS] // XS == iota((GROUPS, ZS), 1)).astype(f32).astype(bf16)
    most = jnp.zeros((1, 1), f32)
    for parity in range(2):
        load = lax.dot_general(
            plane, (counts[parity] == 2.0).astype(f32).astype(bf16), along_cols,
            preferred_element_type=f32,
        )
        most = jnp.maximum(most, jnp.max(jnp.max(load, axis=1, keepdims=True), axis=0, keepdims=True))
    ok_ref[...] = jnp.broadcast_to((most < 1.5).astype(i32), (8, 128))

    @pl.loop(1, ZS)
    def _(t):
        lab_z_arrival(t).wait_recv()

    def add_marks(g, total):
        return total + jnp.where(place[pl.ds(g, 1), :] == group, marks[g], 0)

    label = lax.fori_loop(0, GROUPS, add_marks, jnp.zeros((1, 128), i32))

    def label_at(q):
        return jnp.sum(jnp.where(lane == q, label, 0), axis=1, keepdims=True)

    joined_prev = jnp.logical_and(label_at(pair - 1) == label_at(pair), pair > 0)
    joined_next = jnp.logical_and(label_at(pair + 1) == label_at(pair), pair < PAIRS - 1)
    sides[0] = jnp.broadcast_to(joined_prev.astype(f32), (8, 128))
    sides[1] = jnp.broadcast_to(joined_next.astype(f32), (8, 128))

    def x_out(b, j, kind):
        two = pl.ds(b * BATCH, BATCH)
        to = x_peer(j)
        source = zland.at[two, XS if kind else to]
        return pltpu.make_async_remote_copy(
            source, own.at[two, x, kind], x_send.at[b, j, kind], x_recv.at[b, j, kind],
            device_id=at(z, to), device_id_type=MESH,
        )

    def y_out(b, side):
        two = pl.ds(b * BATCH, BATCH)
        return pltpu.make_async_remote_copy(
            own.at[two], beside.at[side, two], y_send.at[b, side], y_recv.at[b, side],
            device_id=(group, pair_peer(side)), device_id_type=MESH,
        )

    def own_docs(b):
        return own[pl.ds(b * BATCH, BATCH)].reshape(16, SUB, LANE)

    @pl.loop(0, BATCHES + 2)
    def _(s):
        @pl.when(s < BATCHES)
        def _():
            b = s

            @pl.when(b > 0)
            def _():
                z_in(2 * b).wait_recv()

            z_in(2 * b + 1).wait_recv()
            for j in range(1, XS):
                for kind in range(2):
                    x_out(b, j, kind).start()
            for k in range(BATCH):
                own[b * BATCH + k, x, 0] = zland[b * BATCH + k, x]
                own[b * BATCH + k, x, 1] = zland[b * BATCH + k, XS]

        @pl.when(jnp.logical_and(s >= 1, s <= BATCHES))
        def _():
            b = s - 1
            for j in range(1, XS):
                for kind in range(2):
                    x_out(b, j, kind).wait_recv()
            for side in range(2):
                y_out(b, side).start()
            put_wide(wide, 0, own_docs(b))

            @pl.loop(0, SUB)
            def _(c):
                rows[c, pl.ds(pl.multiple_of(b * 16, 16), 16), :] = gather(wide, c, 16).astype(bf16)

        @pl.when(s >= 2)
        def _():
            b = s - 2
            for side in range(2):
                y_out(b, side).wait_recv()
            two = pl.ds(b * BATCH, BATCH)
            use_prev = jnp.broadcast_to(sides[0][0:1, :], (8, 128)) > 0.5
            use_prev = jnp.concatenate([use_prev[0:1].astype(f32)] * 2, axis=1)
            prev = beside[0, two].reshape(16 * SUB, LANE).astype(f32)
            nxt = beside[1, two].reshape(16 * SUB, LANE).astype(f32)
            chosen = jnp.where(jnp.broadcast_to(use_prev, (16 * SUB, LANE)) > 0.5, prev, nxt)
            put_wide(wide, 0, chosen.reshape(16, SUB, LANE))

            @pl.loop(0, SUB)
            def _(c):
                rows[c, pl.ds(pl.multiple_of(BLOCK + b * 16, 16), 16), :] = gather(wide, c, 16).astype(bf16)

    def add_scores(c, total):
        both_rows = rows[c]
        return total + lax.dot_general(
            both_rows[:BLOCK], both_rows, along_rows, preferred_element_type=f32
        )

    scores = lax.fori_loop(0, SUB, add_scores, jnp.zeros((BLOCK, 2 * BLOCK), f32))
    apart = (iota((BLOCK, BLOCK), 0) != iota((BLOCK, BLOCK), 1)).astype(f32)
    prev_mask = lives[1][0:1, :] * sides[0][0:1, :]
    next_mask = lives[2][0:1, :] * sides[1][0:1, :]
    mask = jnp.concatenate(
        [lives[0][0:1, :] * apart, jnp.broadcast_to(prev_mask + next_mask, (BLOCK, BLOCK))], axis=1
    )
    raw = jnp.exp(score_scale * scores) * mask
    weights[...] = raw.astype(bf16)
    denom = self_weight + jnp.sum(raw, axis=1, keepdims=True)
    scale = jnp.broadcast_to(math.sqrt(WIDTH) / denom, (BLOCK, LANE))

    @pl.loop(0, SUB)
    def _(c):
        both_rows = rows[c]
        numer = self_weight * both_rows[:BLOCK].astype(f32) + jnp.dot(
            weights[...], both_rows, preferred_element_type=f32
        )
        spread(wide, c, BLOCK, numer * scale)

    def x_back(b, j, kind):
        two = pl.ds(b * BATCH, BATCH)
        to = x_peer(j)
        target = cand.at[two, x] if kind else zback.at[two, x]
        return pltpu.make_async_remote_copy(
            outd.at[two, to, kind], target, xb_send.at[b, j, kind], xb_recv.at[b, j, kind],
            device_id=at(z, to), device_id_type=MESH,
        )

    def z_home(t):
        return pltpu.make_async_remote_copy(
            zback.at[t], zret.at[mirror(t)], zb_send.at[t], zb_recv.at[mirror(t)],
            device_id=at(z_peer(t), x), device_id_type=MESH,
        )

    def z_arrival(t):
        return pltpu.make_async_remote_copy(
            zback.at[t], zret.at[t], zb_send.at[t], zb_recv.at[t],
            device_id=at(z_peer(t), x), device_id_type=MESH,
        )

    def choose(t):
        chosen = cand[t, XS - 1]
        for k in range(XS - 1):
            flag = choice[pl.ds(t * XS + k, 1), :]
            flag = jnp.broadcast_to(jnp.concatenate([flag, flag], axis=1), (SUB, LANE))
            chosen = jnp.where(flag > 0.5, cand[t, k].astype(f32), chosen.astype(f32)).astype(bf16)
        zback[t, XS] = chosen

    @pl.loop(0, BATCHES + 1)
    def _(s):
        @pl.when(s < BATCHES)
        def _():
            b = s
            for k in range(BATCH):
                t = b * BATCH + k
                outd[t] = docs_of(wide, t * 2 * XS, 2 * XS).reshape(XS, 2, SUB, LANE)
            for j in range(1, XS):
                for kind in range(2):
                    x_back(b, j, kind).start()
            for k in range(BATCH):
                t = b * BATCH + k
                zback[t, x] = outd[t, x, 0]
                cand[t, x] = outd[t, x, 1]

        @pl.when(s >= 1)
        def _():
            b = s - 1
            for j in range(1, XS):
                for kind in range(2):
                    x_back(b, j, kind).wait_recv()
            for k in range(BATCH):
                choose(b * BATCH + k)

            @pl.when(b > 0)
            def _():
                z_home(2 * b).start()

            z_home(2 * b + 1).start()

    put_wide(wide, 0, zback[0])

    @pl.loop(1, ZS)
    def _(t):
        z_arrival(t).wait_recv()
        put_wide(wide, t * SLOTS, zret[t])

    @pl.loop(0, SUB)
    def _(c):
        got = gather(wide, c, SENT).astype(bf16)
        out_ref[:, pl.ds(pl.multiple_of(c * LANE, LANE), LANE)] = jnp.dot(
            unpick[...], got, preferred_element_type=f32
        ).astype(bf16)

    for j in range(1, XS):
        lab_x(j).wait_send()

    @pl.loop(1, ZS)
    def _(t):
        lab_z(t).wait_send()
        z_out(t).wait_send()
        z_home(t).wait_send()

    @pl.loop(0, BATCHES)
    def _(b):
        for j in range(1, XS):
            for kind in range(2):
                x_out(b, j, kind).wait_send()
                x_back(b, j, kind).wait_send()
        for side in range(2):
            y_out(b, side).wait_send()


def put_wide(wide, first, docs):
    n = docs.shape[0]
    flat = docs.astype(f32).reshape(n * SUB, LANE)
    for h in range(2):
        wide[h, pl.ds(pl.multiple_of(first * SUB, SUB), n * SUB), :] = flat[:, h * 128 : (h + 1) * 128]


def docs_of(wide, first, n):
    at = pl.ds(pl.multiple_of(first * SUB, SUB), n * SUB)
    flat = jnp.concatenate([wide[0, at, :], wide[1, at, :]], axis=1)
    return flat.astype(bf16).reshape(n, SUB, LANE)


def spread(wide, c, n, values):
    for h in range(2):
        wide[h, pl.ds(c, n, stride=SUB), :] = values[:, h * 128 : (h + 1) * 128]


def gather(wide, c, n):
    return jnp.concatenate([wide[h, pl.ds(c, n, stride=SUB), :] for h in range(2)], axis=1)


def compact(embeddings, dest, labels):
    vmem = pl.BlockSpec(memory_space=pltpu.VMEM)
    dma = pltpu.SemaphoreType.DMA
    return pl.pallas_call(
        compact_kernel,
        out_shape=(
            jax.ShapeDtypeStruct((COUNT, WIDTH), bf16),
            jax.ShapeDtypeStruct((8, 128), i32),
        ),
        in_specs=[vmem] * 3,
        out_specs=(vmem, vmem),
        scratch_shapes=[
            pltpu.VMEM((COUNT, WIDTH), bf16),
            pltpu.VMEM((2, BLOCK * SUB, 128), f32),
            pltpu.VMEM((ZS, SLOTS, SUB, LANE), bf16),
            pltpu.VMEM((ZS, SLOTS, SUB, LANE), bf16),
            pltpu.VMEM((ZS, XS, 2, SUB, LANE), bf16),
            pltpu.VMEM((2, ZS, XS, 2, SUB, LANE), bf16),
            pltpu.VMEM((SUB, 2 * BLOCK, LANE), bf16),
            pltpu.VMEM((ZS, XS, 2, SUB, LANE), bf16),
            pltpu.VMEM((ZS, SLOTS, SUB, LANE), bf16),
            pltpu.VMEM((ZS, XS, SUB, LANE), bf16),
            pltpu.VMEM((ZS, SLOTS, SUB, LANE), bf16),
            pltpu.VMEM((1, 128), i32),
            pltpu.VMEM((GROUPS, 1, 128), i32),
            pltpu.VMEM((2, GROUPS, 256), f32),
            pltpu.VMEM((GROUPS, 128), i32),
            pltpu.VMEM((SENT, COUNT), bf16),
            pltpu.VMEM((COUNT, SENT), bf16),
            pltpu.VMEM((2, 8, 128), f32),
            pltpu.VMEM((3, 8, BLOCK), f32),
            pltpu.VMEM((GROUPS, 128), f32),
            pltpu.VMEM((BLOCK, 2 * BLOCK), bf16),
            dma((XS,)), dma((XS,)), dma((ZS,)), dma((ZS,)), dma((ZS,)), dma((ZS,)),
            dma((BATCHES, XS, 2)), dma((BATCHES, XS, 2)), dma((BATCHES, 2)), dma((BATCHES, 2)),
            dma((BATCHES, XS, 2)), dma((BATCHES, XS, 2)), dma((ZS,)), dma((ZS,)),
        ],
        compiler_params=pltpu.CompilerParams(
            collective_id=0, has_side_effects=True, vmem_limit_bytes=40 << 20
        ),
    )(embeddings, dest, labels)


def on_device(embeddings, dest, labels):
    out, ok = compact(embeddings, dest.reshape(GROUPS * PAIRS * COUNT // 128, 128), labels)
    return lax.cond(ok[0, 0] == 1, lambda: out, lambda: padded(embeddings, dest, labels))


def solution(mesh):
    in_specs = (P(("group", "pair"), None), P(), P("group", None))
    out_specs = P(("group", "pair"), None)
    return jax.shard_map(
        on_device, mesh=mesh, in_specs=in_specs, out_specs=out_specs, check_vma=False
    )
```

```python
import math

import jax
import jax.numpy as jnp
from jax import lax
from jax.experimental import pallas as pl
from jax.experimental.pallas import tpu as pltpu
from jax.sharding import PartitionSpec as P

score_scale = 64.0
self_weight = math.exp(4.0)
along_rows = (((1,), (1,)), ((), ()))
along_cols = (((0,), (0,)), ((), ()))


def shifted(block, axis, distance):
    devices = range(lax.axis_size(axis))
    route = [(i - distance, i) for i in devices if i - distance in devices]
    return lax.ppermute(block, axis, route)


def normalized(rows):
    values = rows.astype(jnp.float32)
    factor = lax.rsqrt(jnp.mean(values * values, axis=-1, keepdims=True) + 1e-05)
    return (values * factor * (1.0 / math.sqrt(values.shape[-1]))).astype(jnp.bfloat16)


def live_slots(routes, source_pair, owner, capacity):
    column = lax.dynamic_index_in_dim(routes, source_pair, axis=1, keepdims=False)
    counts = jnp.sum((column == owner).astype(jnp.int32), axis=1)
    return (
        (jnp.arange(capacity, dtype=jnp.int32)[None, :] < counts[:, None])
        .reshape(-1)
        .astype(jnp.float32)
    )


def pair_weights(left, right, mask):
    scores = lax.dot_general(left, right, along_rows, preferred_element_type=jnp.float32)
    return jnp.exp(score_scale * scores) * mask


def padded(embeddings, dest, labels):
    groups = lax.axis_size("group")
    pairs = lax.axis_size("pair")
    group_at = lax.axis_index("group")
    pair_at = lax.axis_index("pair")
    count = embeddings.shape[0]
    width = embeddings.shape[1]
    capacity = 2 * count // groups
    slots = groups * capacity
    routes = dest.reshape(groups, pairs, count)
    own_routes = lax.dynamic_index_in_dim(
        lax.dynamic_index_in_dim(routes, group_at, axis=0, keepdims=False),
        pair_at,
        axis=0,
        keepdims=False,
    )
    hits = (own_routes[:, None] == jnp.arange(groups, dtype=jnp.int32)[None, :]).astype(jnp.int32)
    ranks = jnp.sum(jnp.cumsum(hits, axis=0) * hits, axis=1) - 1
    slot = own_routes * capacity + ranks
    match = (slot[None, :] == jnp.arange(slots, dtype=jnp.int32)[:, None]).astype(jnp.int32)
    slot_doc = jnp.sum(match * jnp.arange(count, dtype=jnp.int32)[None, :], axis=1)
    filled = jnp.sum(match, axis=1)
    hat = normalized(embeddings)
    outgoing = jnp.where(filled[:, None] > 0, hat[slot_doc], jnp.zeros((), jnp.bfloat16))
    arrived = lax.all_to_all(
        outgoing.reshape(groups, capacity, width), "group", split_axis=0, concat_axis=0, tiled=True
    )
    block = arrived.reshape(slots, width)
    marks = labels[0]
    mine = marks[pair_at]
    live_mine = live_slots(routes, pair_at, group_at, capacity)
    next_at = jnp.minimum(pair_at + 1, pairs - 1)
    joined_next = jnp.logical_and(pair_at + 1 < pairs, marks[next_at] == mine).astype(jnp.float32)
    live_next = live_slots(routes, next_at, group_at, capacity)
    apart = (jnp.arange(slots)[:, None] != jnp.arange(slots)[None, :]).astype(jnp.float32)
    own_weights = pair_weights(block, block, live_mine[None, :] * apart)
    numer = self_weight * block.astype(jnp.float32) + jnp.dot(
        own_weights.astype(jnp.bfloat16), block, preferred_element_type=jnp.float32
    )
    denom = self_weight + jnp.sum(own_weights, axis=1)
    neighbour = shifted(block, "pair", -1)
    next_weights = pair_weights(
        block, neighbour, live_mine[:, None] * live_next[None, :] * joined_next
    )
    next_rounded = next_weights.astype(jnp.bfloat16)
    numer = numer + jnp.dot(next_rounded, neighbour, preferred_element_type=jnp.float32)
    denom = denom + jnp.sum(next_weights, axis=1)
    column_numer = lax.dot_general(
        next_rounded, block, along_cols, preferred_element_type=jnp.float32
    )
    column_denom = jnp.sum(next_weights, axis=0)
    came_numer, came_denom = (
        shifted(column_numer.astype(jnp.bfloat16), "pair", 1).astype(column_numer.dtype),
        shifted(column_denom.astype(jnp.bfloat16), "pair", 1).astype(column_denom.dtype),
    )
    numer = numer + came_numer
    denom = denom + came_denom
    block_out = (math.sqrt(width) * numer / denom[:, None]).astype(jnp.bfloat16)
    returned = lax.all_to_all(
        block_out.reshape(groups, capacity, width), "group", split_axis=0, concat_axis=0, tiled=True
    )
    return returned.reshape(slots, width)[slot]


ZS, XS, PAIRS, COUNT, WIDTH = 16, 4, 8, 64, 4096
GROUPS = ZS * XS
SUB, LANE = 16, 256
BLOCK = GROUPS * 2
SENT = GROUPS + ZS
BATCH = 2
BATCHES = ZS // BATCH
QUAD = 4
QUADS = ZS // QUAD
AHEAD = 3
UNROLL = 4
MESH = pl.DeviceIdType.MESH
f32, bf16, i32 = jnp.float32, jnp.bfloat16, jnp.int32


def distance_at(t):
    half = t // 2
    far = jnp.where(t % 2 == 0, 8 - half, 8 + half)
    return jnp.where(t == 0, 0, far)


def step_of(distance):
    near = jnp.where(distance < 8, 16 - 2 * distance, 2 * distance - 15)
    return jnp.where(distance == 0, 0, near)


def mirror(t):
    return jnp.where(t < 2, t, jnp.where(t % 2 == 0, t + 1, t - 1))


def iota(shape, axis):
    return lax.broadcasted_iota(i32, shape, axis)


def put_wide(wide, first, docs):
    n = docs.shape[0]
    flat = docs.astype(f32).reshape(n * SUB, LANE)
    for h in range(2):
        wide[h, pl.ds(pl.multiple_of(first * SUB, SUB), n * SUB), :] = flat[:, h * 128 : (h + 1) * 128]


def docs_of(wide, first, n):
    at = pl.ds(pl.multiple_of(first * SUB, SUB), n * SUB)
    flat = jnp.concatenate([wide[0, at, :], wide[1, at, :]], axis=1)
    return flat.astype(bf16).reshape(n, SUB, LANE)


def spread(wide, c, first, n, values):
    for h in range(2):
        wide[h, pl.ds(first * SUB + c, n, stride=SUB), :] = values[:, h * 128 : (h + 1) * 128]


def gather(wide, c, n):
    return jnp.concatenate([wide[h, pl.ds(c, n, stride=SUB), :] for h in range(2)], axis=1)


def chunk(c):
    return pl.ds(pl.multiple_of(c * LANE, LANE), LANE)


def compact_kernel(
    x_ref, dest_ref, lab_ref, out_ref, ok_ref,
    xv, hat, wide, send_r, send_s, land_s, own, beside, rows, out_r, out_s, back_s, cand, ret_r, ret_s,
    mark, marks, counts, place, pick, unpick, sides, lives, choice, weights, scores,
    in_sem, lab_x_send, lab_x_recv, lab_z_send, lab_z_recv,
    r_send, r_recv, s_send, s_recv, m_send, m_recv, yr_send, yr_recv, ys_send, ys_recv,
    rb_send, rb_recv, mb_send, mb_recv, sb_send, sb_recv,
):
    group = lax.axis_index("group")
    pair = lax.axis_index("pair")
    z, x = group // XS, group % XS

    def at(zz, xx):
        return (zz * XS + xx, pair)

    def z_peer(t):
        return lax.rem(z + distance_at(t), ZS)

    def x_peer(j):
        return lax.rem(x + j, XS)

    def pair_peer(side):
        return lax.rem(pair + jnp.where(side == 0, 1, PAIRS - 1), PAIRS)

    def remote(source, target, send, recv, device):
        return pltpu.make_async_remote_copy(
            source, target, send, recv, device_id=device, device_id_type=MESH
        )

    barrier = pltpu.get_barrier_semaphore()

    @pl.loop(1, GROUPS)
    def _(d):
        pl.semaphore_signal(
            barrier, inc=1, device_id=(lax.rem(group + d, GROUPS), pair), device_id_type=MESH
        )

    for step in (1, PAIRS - 1):
        pl.semaphore_signal(
            barrier, inc=1, device_id=(group, lax.rem(pair + step, PAIRS)), device_id_type=MESH
        )

    load_x = pltpu.make_async_copy(x_ref, xv, in_sem)
    load_x.start()

    turned = dest_ref[...].T
    for parity in range(2):
        part = turned[parity * COUNT : (parity + 1) * COUNT, :]
        unit = jnp.left_shift(jnp.ones_like(part), (part & 7) * 4)
        for k in range(GROUPS // 8):
            held = jnp.sum(jnp.where((part >> 3) == k, unit, 0), axis=0, keepdims=True)
            nibble = jnp.broadcast_to(held, (8, 256)) >> (iota((8, 256), 0) * 4)
            counts[parity, 8 * k : 8 * k + 8, :] = (nibble & 3).astype(f32)
    second = [(counts[parity] == 2.0).astype(f32) for parity in range(2)]
    both = (second[0] + second[1]).astype(bf16)
    need_col = jnp.sum(second[0] + second[1], axis=1, keepdims=True)
    need_row = lax.dot_general(
        jnp.ones((8, 256), bf16), both, along_rows, preferred_element_type=f32
    )[0:1, :]
    g_col, g_row = iota((GROUPS, GROUPS), 0), iota((GROUPS, GROUPS), 1)
    ahead = jnp.logical_or(
        need_row > need_col, jnp.logical_and(need_row == need_col, g_row < g_col)
    )
    standing = jnp.sum(ahead.astype(i32), axis=1, keepdims=True)
    position = (standing % ZS) * XS + standing // ZS
    place[...] = jnp.broadcast_to(position, (GROUPS, 128))

    cell = group * (PAIRS // 2) + pair // 2
    line = dest_ref[pl.ds(cell, 1), :]
    lane = iota((1, 128), 1)
    mine = lane // COUNT == pair % 2
    line = jnp.where(mine, line, -1)
    eye = iota((128, 128), 0) == iota((128, 128), 1)
    line_col = jnp.sum(jnp.where(eye, jnp.broadcast_to(line, (128, 128)), 0), axis=1, keepdims=True)
    earlier = jnp.logical_and(line_col == line, iota((128, 128), 0) < iota((128, 128), 1))
    rank = jnp.sum(earlier.astype(i32), axis=0, keepdims=True)
    spot = jnp.sum(
        jnp.where(iota((GROUPS, 128), 0) == line, place[...], 0), axis=0, keepdims=True
    )
    step = step_of((spot // XS - z + ZS) % ZS)
    slot = jnp.where(rank == 0, step * XS + spot % XS, GROUPS + step)
    slot = jnp.where(mine, slot, -1)
    fold = slot[:, :COUNT] + slot[:, COUNT:] + 1
    slot_col = jnp.sum(
        jnp.where(
            iota((COUNT, COUNT), 0) == iota((COUNT, COUNT), 1),
            jnp.broadcast_to(fold, (COUNT, COUNT)),
            0,
        ),
        axis=1,
        keepdims=True,
    )
    pick[...] = (iota((SENT, COUNT), 0) == fold).astype(f32).astype(bf16)
    unpick[...] = (iota((COUNT, SENT), 1) == slot_col).astype(f32).astype(bf16)
    mark[...] = jnp.zeros((1, 128), i32)
    mark[:, 0:PAIRS] = lab_ref[...]
    marks[pl.ds(group, 1), :, :] = mark[...].reshape(1, 1, 128)

    load_x.wait()

    @pl.loop(0, COUNT // 16)
    def _(i):
        r = pl.ds(pl.multiple_of(i * 16, 16), 16)
        values = xv[r, :].astype(f32)
        factor = lax.rsqrt(jnp.mean(values * values, axis=-1, keepdims=True) + 1e-05)
        hat[r, :] = (values * factor * (1.0 / math.sqrt(WIDTH))).astype(bf16)

    @pl.loop(0, SUB, unroll=UNROLL)
    def _(c):
        got = jnp.dot(pick[...], hat[:, chunk(c)], preferred_element_type=f32)
        spread(wide, c, 0, SENT, got)

    send_s[...] = docs_of(wide, GROUPS, ZS)

    def lab_x(j, source):
        here = marks.at[pl.ds(z * XS + source, 1)]
        return remote(here, here, lab_x_send.at[j], lab_x_recv.at[j], at(z, x_peer(j)))

    def lab_z(t, plane, slot):
        here = marks.at[pl.ds(plane * XS, XS)]
        return remote(here, here, lab_z_send.at[t], lab_z_recv.at[slot], at(z_peer(t), x))

    def r_out(t, j):
        to = x_peer(j)
        return remote(
            send_r.at[t, to], own.at[0, mirror(t), x], r_send.at[t, j], r_recv.at[mirror(t), j],
            at(z_peer(t), to),
        )

    def r_in(t, j):
        source = lax.rem(x + XS - j, XS)
        return remote(
            send_r.at[t, source], own.at[0, t, source], r_send.at[t, j], r_recv.at[t, j],
            at(z_peer(t), x_peer(j)),
        )

    def s_out(t, slot):
        return remote(send_s.at[t], land_s.at[slot], s_send.at[t], s_recv.at[slot], at(z_peer(t), x))

    def s_share(k, j, source):
        four = pl.ds(k * QUAD, QUAD)
        return remote(
            land_s.at[four], own.at[1, four, source], m_send.at[k, j], m_recv.at[k, j],
            at(z, x_peer(j)),
        )

    def yr_out(b, side):
        two = pl.ds(b * BATCH, BATCH)
        return remote(
            own.at[0, two], beside.at[side, 0, two], yr_send.at[b, side], yr_recv.at[b, side],
            (group, pair_peer(side)),
        )

    def ys_out(k, side):
        four = pl.ds(k * QUAD, QUAD)
        return remote(
            own.at[1, four], beside.at[side, 1, four], ys_send.at[k, side], ys_recv.at[k, side],
            (group, pair_peer(side)),
        )

    def r_batch(b, act):
        for k in range(BATCH):
            t = b * BATCH + k
            for j in range(XS):
                if j == 0 and k == 0:
                    @pl.when(t > 0)
                    def _():
                        act(t, j)
                else:
                    act(t, j)

    pl.semaphore_wait(barrier, GROUPS - 1 + 2)

    for j in range(1, XS):
        lab_x(j, x).start()

    @pl.loop(1, ZS)
    def _(t):
        s_out(t, mirror(t)).start()

    land_s[0] = send_s[0]

    @pl.loop(0, BATCHES)
    def _(b):
        two = pl.ds(b * BATCH, BATCH)
        send_r[two] = docs_of(wide, b * BATCH * XS, BATCH * XS).reshape(BATCH, XS, SUB, LANE)

        @pl.when(b < AHEAD)
        def _():
            r_batch(b, lambda t, j: r_out(t, j).start())

    own[0, 0, x] = send_r[0, x]

    for j in range(1, XS):
        lab_x(j, lax.rem(x + XS - j, XS)).wait_recv()

    @pl.loop(1, ZS)
    def _(t):
        lab_z(t, z, mirror(t)).start()

    @pl.loop(0, QUADS)
    def _(k):
        for i in range(QUAD):
            t = k * QUAD + i
            if i == 0:
                @pl.when(t > 0)
                def _():
                    s_out(t, t).wait_recv()
            else:
                s_out(t, t).wait_recv()
        for j in range(1, XS):
            s_share(k, j, x).start()
        for i in range(QUAD):
            own[1, k * QUAD + i, x] = land_s[k * QUAD + i]

    here = place[:, 0:1] == group
    held = [
        jnp.sum(jnp.where(here, counts[parity], 0.0), axis=0, keepdims=True) for parity in range(2)
    ]
    s_lane = iota((256, BLOCK), 1)
    s_source = lax.rem(z + distance_at((s_lane // XS) % ZS), ZS) * XS + s_lane % XS
    for n, shift in enumerate((0, PAIRS - 1, 1)):
        other = lax.rem(pair + shift, PAIRS)
        row = jnp.where(other % 2 == 0, held[0], held[1])
        chosen = (iota((256, BLOCK), 0) == s_source * (PAIRS // 2) + other // 2).astype(f32)
        filled = jnp.dot(
            jnp.broadcast_to(row, (8, 256)).astype(bf16), chosen.astype(bf16),
            preferred_element_type=f32,
        )
        lives[n] = (filled > (iota((8, BLOCK), 1) // GROUPS).astype(f32)).astype(f32)

    at_here = (place[:, 0:GROUPS] == z * XS + iota((GROUPS, GROUPS), 1) % XS).astype(f32)
    wanted = jnp.where(
        pair % 2 == 0, (counts[0] == 2.0).astype(f32), (counts[1] == 2.0).astype(f32)
    )
    owner_of = lax.dot_general(
        at_here.astype(bf16), wanted.astype(bf16), along_cols, preferred_element_type=f32
    )
    t_row = iota((GROUPS, 256), 0) // XS
    c_row = (lax.rem(z + distance_at(t_row), ZS) * XS + x) * (PAIRS // 2) + pair // 2
    choice[...] = jnp.broadcast_to(
        jnp.sum(jnp.where(iota((GROUPS, 256), 1) == c_row, owner_of, 0.0), axis=1, keepdims=True),
        (GROUPS, 128),
    )

    plane = (place[:, 0:ZS] // XS == iota((GROUPS, ZS), 1)).astype(f32).astype(bf16)
    most = jnp.zeros((1, 1), f32)
    for parity in range(2):
        load = lax.dot_general(
            plane, (counts[parity] == 2.0).astype(f32).astype(bf16), along_cols,
            preferred_element_type=f32,
        )
        most = jnp.maximum(most, jnp.max(jnp.max(load, axis=1, keepdims=True), axis=0, keepdims=True))
    ok_ref[...] = (most < 1.5).astype(i32)

    def read_labels():
        @pl.loop(1, ZS)
        def _(t):
            lab_z(t, z_peer(t), t).wait_recv()

        def add_marks(g, total):
            return total + jnp.where(place[pl.ds(g, 1), :] == group, marks[g], 0)

        label = lax.fori_loop(0, GROUPS, add_marks, jnp.zeros((1, 128), i32))

        def label_at(q):
            return jnp.sum(jnp.where(lane == q, label, 0), axis=1, keepdims=True)

        joined_prev = jnp.logical_and(label_at(pair - 1) == label_at(pair), pair > 0)
        joined_next = jnp.logical_and(label_at(pair + 1) == label_at(pair), pair < PAIRS - 1)
        sides[0] = jnp.broadcast_to(joined_prev.astype(f32), (8, 128))
        sides[1] = jnp.broadcast_to(joined_next.astype(f32), (8, 128))

    def to_rows(first):
        @pl.loop(0, SUB, unroll=UNROLL)
        def _(c):
            rows[c, pl.ds(pl.multiple_of(first, 16), 16), :] = gather(wide, c, 16).astype(bf16)

    def own_rows(kind, k):
        put_wide(wide, 0, own[kind, pl.ds(k * QUAD, QUAD)].reshape(16, SUB, LANE))
        to_rows(kind * GROUPS + k * 16)

    def beside_rows(kind, k):
        four = pl.ds(k * QUAD, QUAD)
        flag = sides[0][0:1, :]
        flag = jnp.broadcast_to(jnp.concatenate([flag, flag], axis=1), (16 * SUB, LANE))
        prev = beside[0, kind, four].reshape(16 * SUB, LANE).astype(f32)
        nxt = beside[1, kind, four].reshape(16 * SUB, LANE).astype(f32)
        put_wide(wide, 0, jnp.where(flag > 0.5, prev, nxt).reshape(16, SUB, LANE))
        to_rows(BLOCK + kind * GROUPS + k * 16)

    @pl.loop(0, QUADS)
    def _(k):
        for j in range(1, XS):
            s_share(k, j, lax.rem(x + XS - j, XS)).wait_recv()
        for side in range(2):
            ys_out(k, side).start()

    @pl.loop(0, BATCHES)
    def _(b):
        r_batch(b, lambda t, j: r_in(t, j).wait_recv())

        @pl.when(b + AHEAD < BATCHES)
        def _():
            r_batch(b + AHEAD, lambda t, j: r_out(t, j).start())

        for side in range(2):
            yr_out(b, side).start()

        @pl.when(b % 2 == 1)
        def _():
            own_rows(0, b // 2)
            own_rows(1, b // 2)

        pl.when(b == 3)(read_labels)

        @pl.when(b >= 4)
        def _():
            k = b - 4
            for side in range(2):
                ys_out(k, side).wait_recv()
            beside_rows(1, k)

    def add_own(c, total):
        mine = rows[c, 0:BLOCK]
        return total + lax.dot_general(mine, mine, along_rows, preferred_element_type=f32)

    scores[:, 0:BLOCK] = lax.fori_loop(
        0, SUB, add_own, jnp.zeros((BLOCK, BLOCK), f32), unroll=UNROLL
    )

    @pl.loop(0, QUADS)
    def _(k):
        for i in range(2):
            for side in range(2):
                yr_out(2 * k + i, side).wait_recv()
        beside_rows(0, k)

    prev_mask = lives[1][0:1, :] * sides[0][0:1, :]
    next_mask = lives[2][0:1, :] * sides[1][0:1, :]
    side_mask = jnp.broadcast_to(prev_mask + next_mask, (GROUPS, BLOCK))

    def smooth(kind):
        part = pl.ds(kind * GROUPS, GROUPS)

        def add_side(c, total):
            return total + lax.dot_general(
                rows[c, part], rows[c, BLOCK : 2 * BLOCK], along_rows, preferred_element_type=f32
            )

        scores[part, BLOCK : 2 * BLOCK] = lax.fori_loop(
            0, SUB, add_side, jnp.zeros((GROUPS, BLOCK), f32), unroll=UNROLL
        )
        apart = (iota((GROUPS, BLOCK), 0) + kind * GROUPS != iota((GROUPS, BLOCK), 1)).astype(f32)
        mask = jnp.concatenate([lives[0][0:1, :] * apart, side_mask], axis=1)
        raw = jnp.exp(score_scale * scores[part, :]) * mask
        weights[...] = raw.astype(bf16)
        denom = self_weight + jnp.sum(raw, axis=1, keepdims=True)
        scale = jnp.broadcast_to(math.sqrt(WIDTH) / denom, (GROUPS, LANE))

        @pl.loop(0, SUB, unroll=UNROLL)
        def _(c):
            numer = self_weight * rows[c, part].astype(f32) + jnp.dot(
                weights[...], rows[c], preferred_element_type=f32
            )
            spread(wide, c, kind * GROUPS, GROUPS, numer * scale)

    def r_home(t, j):
        to = x_peer(j)
        return remote(
            out_r.at[t, to], ret_r.at[mirror(t), x], rb_send.at[t, j], rb_recv.at[mirror(t), j],
            at(z_peer(t), to),
        )

    def r_arrival(t, j):
        source = lax.rem(x + XS - j, XS)
        return remote(
            out_r.at[t, source], ret_r.at[t, source], rb_send.at[t, j], rb_recv.at[t, j],
            at(z_peer(t), x_peer(j)),
        )

    def s_back(k, j, to, target):
        four = pl.ds(k * QUAD, QUAD)
        return remote(
            out_s.at[four, to], cand.at[four, target], mb_send.at[k, j], mb_recv.at[k, j],
            at(z, x_peer(j)),
        )

    def s_home(t, slot):
        return remote(back_s.at[t], ret_s.at[slot], sb_send.at[t], sb_recv.at[slot], at(z_peer(t), x))

    smooth(0)

    @pl.loop(0, BATCHES)
    def _(b):
        two = pl.ds(b * BATCH, BATCH)
        out_r[two] = docs_of(wide, b * BATCH * XS, BATCH * XS).reshape(BATCH, XS, SUB, LANE)
        r_batch(b, lambda t, j: r_home(t, j).start())

    ret_r[0, x] = out_r[0, x]

    smooth(1)

    @pl.loop(0, QUADS)
    def _(k):
        four = pl.ds(k * QUAD, QUAD)
        out_s[four] = docs_of(wide, GROUPS + k * 16, 16).reshape(QUAD, XS, SUB, LANE)
        for j in range(1, XS):
            s_back(k, j, x_peer(j), x).start()
        for i in range(QUAD):
            cand[k * QUAD + i, x] = out_s[k * QUAD + i, x]

    def choose(t):
        chosen = cand[t, XS - 1].astype(f32)
        for k in range(XS - 1):
            flag = choice[pl.ds(t * XS + k, 1), :]
            flag = jnp.broadcast_to(jnp.concatenate([flag, flag], axis=1), (SUB, LANE))
            chosen = jnp.where(flag > 0.5, cand[t, k].astype(f32), chosen)
        back_s[t] = chosen.astype(bf16)

    @pl.loop(0, QUADS)
    def _(k):
        for j in range(1, XS):
            s_back(k, j, x, lax.rem(x + XS - j, XS)).wait_recv()
        for i in range(QUAD):
            t = k * QUAD + i
            choose(t)
            if i == 0:
                @pl.when(t > 0)
                def _():
                    s_home(t, mirror(t)).start()
            else:
                s_home(t, mirror(t)).start()

    ret_s[0] = back_s[0]

    @pl.loop(0, BATCHES)
    def _(b):
        r_batch(b, lambda t, j: r_arrival(t, j).wait_recv())
        two = pl.ds(b * BATCH, BATCH)
        put_wide(wide, b * BATCH * XS, ret_r[two].reshape(BATCH * XS, SUB, LANE))

    @pl.loop(1, ZS)
    def _(t):
        s_home(t, t).wait_recv()

    put_wide(wide, GROUPS, ret_s[...])

    @pl.loop(0, SUB, unroll=UNROLL)
    def _(c):
        got = gather(wide, c, SENT).astype(bf16)
        out_ref[:, chunk(c)] = jnp.dot(unpick[...], got, preferred_element_type=f32).astype(bf16)

    for j in range(1, XS):
        lab_x(j, x).wait_send()

    @pl.loop(1, ZS)
    def _(t):
        lab_z(t, z, mirror(t)).wait_send()
        s_out(t, mirror(t)).wait_send()
        s_home(t, mirror(t)).wait_send()

    @pl.loop(0, BATCHES)
    def _(b):
        r_batch(b, lambda t, j: r_out(t, j).wait_send())
        r_batch(b, lambda t, j: r_home(t, j).wait_send())
        for side in range(2):
            yr_out(b, side).wait_send()

    @pl.loop(0, QUADS)
    def _(k):
        for j in range(1, XS):
            s_share(k, j, x).wait_send()
            s_back(k, j, x_peer(j), x).wait_send()
        for side in range(2):
            ys_out(k, side).wait_send()


def compact(embeddings, dest, labels):
    vmem = pl.BlockSpec(memory_space=pltpu.VMEM)
    dma = pltpu.SemaphoreType.DMA
    return pl.pallas_call(
        compact_kernel,
        out_shape=(
            jax.ShapeDtypeStruct((COUNT, WIDTH), bf16),
            jax.ShapeDtypeStruct((1, 1), i32),
        ),
        in_specs=[pl.BlockSpec(memory_space=pl.ANY), vmem, vmem],
        out_specs=(vmem, vmem),
        scratch_shapes=[
            pltpu.VMEM((COUNT, WIDTH), bf16),
            pltpu.VMEM((COUNT, WIDTH), bf16),
            pltpu.VMEM((2, BLOCK * SUB, 128), f32),
            pltpu.VMEM((ZS, XS, SUB, LANE), bf16),
            pltpu.VMEM((ZS, SUB, LANE), bf16),
            pltpu.VMEM((ZS, SUB, LANE), bf16),
            pltpu.VMEM((2, ZS, XS, SUB, LANE), bf16),
            pltpu.VMEM((2, 2, ZS, XS, SUB, LANE), bf16),
            pltpu.VMEM((SUB, 2 * BLOCK, LANE), bf16),
            pltpu.VMEM((ZS, XS, SUB, LANE), bf16),
            pltpu.VMEM((ZS, XS, SUB, LANE), bf16),
            pltpu.VMEM((ZS, SUB, LANE), bf16),
            pltpu.VMEM((ZS, XS, SUB, LANE), bf16),
            pltpu.VMEM((ZS, XS, SUB, LANE), bf16),
            pltpu.VMEM((ZS, SUB, LANE), bf16),
            pltpu.VMEM((1, 128), i32),
            pltpu.VMEM((GROUPS, 1, 128), i32),
            pltpu.VMEM((2, GROUPS, 256), f32),
            pltpu.VMEM((GROUPS, 128), i32),
            pltpu.VMEM((SENT, COUNT), bf16),
            pltpu.VMEM((COUNT, SENT), bf16),
            pltpu.VMEM((2, 8, 128), f32),
            pltpu.VMEM((3, 8, BLOCK), f32),
            pltpu.VMEM((GROUPS, 128), f32),
            pltpu.VMEM((GROUPS, 2 * BLOCK), bf16),
            pltpu.VMEM((BLOCK, 2 * BLOCK), f32),
            dma(()),
            dma((XS,)), dma((XS,)), dma((ZS,)), dma((ZS,)),
            dma((ZS, XS)), dma((ZS, XS)), dma((ZS,)), dma((ZS,)), dma((QUADS, XS)), dma((QUADS, XS)),
            dma((BATCHES, 2)), dma((BATCHES, 2)), dma((QUADS, 2)), dma((QUADS, 2)),
            dma((ZS, XS)), dma((ZS, XS)), dma((QUADS, XS)), dma((QUADS, XS)), dma((ZS,)), dma((ZS,)),
        ],
        compiler_params=pltpu.CompilerParams(
            collective_id=0, has_side_effects=True, vmem_limit_bytes=40 << 20
        ),
    )(embeddings, dest, labels)


def on_device(embeddings, dest, labels):
    out, ok = compact(embeddings, dest.reshape(GROUPS * PAIRS * COUNT // 128, 128), labels)
    return lax.cond(ok.reshape(()) == 1, lambda: out, lambda: padded(embeddings, dest, labels))


def solution(mesh):
    in_specs = (P(("group", "pair"), None), P(), P("group", None))
    out_specs = P(("group", "pair"), None)
    return jax.shard_map(
        on_device, mesh=mesh, in_specs=in_specs, out_specs=out_specs, check_vma=False
    )
```

```python
import math

import jax
import jax.numpy as jnp
from jax import lax
from jax.experimental import pallas as pl
from jax.experimental.pallas import tpu as pltpu
from jax.sharding import PartitionSpec as P

score_scale = 64.0
self_weight = math.exp(4.0)
along_rows = (((1,), (1,)), ((), ()))
along_cols = (((0,), (0,)), ((), ()))


def shifted(block, axis, distance):
    devices = range(lax.axis_size(axis))
    route = [(i - distance, i) for i in devices if i - distance in devices]
    return lax.ppermute(block, axis, route)


def normalized(rows):
    values = rows.astype(jnp.float32)
    factor = lax.rsqrt(jnp.mean(values * values, axis=-1, keepdims=True) + 1e-05)
    return (values * factor * (1.0 / math.sqrt(values.shape[-1]))).astype(jnp.bfloat16)


def live_slots(routes, source_pair, owner, capacity):
    column = lax.dynamic_index_in_dim(routes, source_pair, axis=1, keepdims=False)
    counts = jnp.sum((column == owner).astype(jnp.int32), axis=1)
    return (
        (jnp.arange(capacity, dtype=jnp.int32)[None, :] < counts[:, None])
        .reshape(-1)
        .astype(jnp.float32)
    )


def pair_weights(left, right, mask):
    scores = lax.dot_general(left, right, along_rows, preferred_element_type=jnp.float32)
    return jnp.exp(score_scale * scores) * mask


def padded(embeddings, dest, labels):
    groups = lax.axis_size("group")
    pairs = lax.axis_size("pair")
    group_at = lax.axis_index("group")
    pair_at = lax.axis_index("pair")
    count = embeddings.shape[0]
    width = embeddings.shape[1]
    capacity = 2 * count // groups
    slots = groups * capacity
    routes = dest.reshape(groups, pairs, count)
    own_routes = lax.dynamic_index_in_dim(
        lax.dynamic_index_in_dim(routes, group_at, axis=0, keepdims=False),
        pair_at,
        axis=0,
        keepdims=False,
    )
    hits = (own_routes[:, None] == jnp.arange(groups, dtype=jnp.int32)[None, :]).astype(jnp.int32)
    ranks = jnp.sum(jnp.cumsum(hits, axis=0) * hits, axis=1) - 1
    slot = own_routes * capacity + ranks
    match = (slot[None, :] == jnp.arange(slots, dtype=jnp.int32)[:, None]).astype(jnp.int32)
    slot_doc = jnp.sum(match * jnp.arange(count, dtype=jnp.int32)[None, :], axis=1)
    filled = jnp.sum(match, axis=1)
    hat = normalized(embeddings)
    outgoing = jnp.where(filled[:, None] > 0, hat[slot_doc], jnp.zeros((), jnp.bfloat16))
    arrived = lax.all_to_all(
        outgoing.reshape(groups, capacity, width), "group", split_axis=0, concat_axis=0, tiled=True
    )
    block = arrived.reshape(slots, width)
    marks = labels[0]
    mine = marks[pair_at]
    live_mine = live_slots(routes, pair_at, group_at, capacity)
    next_at = jnp.minimum(pair_at + 1, pairs - 1)
    joined_next = jnp.logical_and(pair_at + 1 < pairs, marks[next_at] == mine).astype(jnp.float32)
    live_next = live_slots(routes, next_at, group_at, capacity)
    apart = (jnp.arange(slots)[:, None] != jnp.arange(slots)[None, :]).astype(jnp.float32)
    own_weights = pair_weights(block, block, live_mine[None, :] * apart)
    numer = self_weight * block.astype(jnp.float32) + jnp.dot(
        own_weights.astype(jnp.bfloat16), block, preferred_element_type=jnp.float32
    )
    denom = self_weight + jnp.sum(own_weights, axis=1)
    neighbour = shifted(block, "pair", -1)
    next_weights = pair_weights(
        block, neighbour, live_mine[:, None] * live_next[None, :] * joined_next
    )
    next_rounded = next_weights.astype(jnp.bfloat16)
    numer = numer + jnp.dot(next_rounded, neighbour, preferred_element_type=jnp.float32)
    denom = denom + jnp.sum(next_weights, axis=1)
    column_numer = lax.dot_general(
        next_rounded, block, along_cols, preferred_element_type=jnp.float32
    )
    column_denom = jnp.sum(next_weights, axis=0)
    came_numer, came_denom = (
        shifted(column_numer.astype(jnp.bfloat16), "pair", 1).astype(column_numer.dtype),
        shifted(column_denom.astype(jnp.bfloat16), "pair", 1).astype(column_denom.dtype),
    )
    numer = numer + came_numer
    denom = denom + came_denom
    block_out = (math.sqrt(width) * numer / denom[:, None]).astype(jnp.bfloat16)
    returned = lax.all_to_all(
        block_out.reshape(groups, capacity, width), "group", split_axis=0, concat_axis=0, tiled=True
    )
    return returned.reshape(slots, width)[slot]


ZS, XS, PAIRS, COUNT, WIDTH = 16, 4, 8, 64, 4096
GROUPS = ZS * XS
SUB, LANE = 16, 256
BLOCK = GROUPS * 2
SENT = GROUPS + ZS
BATCH = 2
BATCHES = ZS // BATCH
QUAD = 4
QUADS = ZS // QUAD
AHEAD = 5
UNROLL = 8
FIRST = 4
MESH = pl.DeviceIdType.MESH
f32, bf16, i32 = jnp.float32, jnp.bfloat16, jnp.int32


def distance_at(t):
    half = t // 2
    far = jnp.where(t % 2 == 0, 8 - half, 8 + half)
    return jnp.where(t == 0, 0, far)


def step_of(distance):
    near = jnp.where(distance < 8, 16 - 2 * distance, 2 * distance - 15)
    return jnp.where(distance == 0, 0, near)


def mirror(t):
    return jnp.where(t < 2, t, jnp.where(t % 2 == 0, t + 1, t - 1))


def iota(shape, axis):
    return lax.broadcasted_iota(i32, shape, axis)


def put_wide(wide, first, docs):
    n = docs.shape[0]
    flat = docs.astype(f32).reshape(n * SUB, LANE)
    for h in range(2):
        wide[h, pl.ds(pl.multiple_of(first * SUB, SUB), n * SUB), :] = flat[:, h * 128 : (h + 1) * 128]


def docs_of(wide, first, n):
    at = pl.ds(pl.multiple_of(first * SUB, SUB), n * SUB)
    flat = jnp.concatenate([wide[0, at, :], wide[1, at, :]], axis=1)
    return flat.astype(bf16).reshape(n, SUB, LANE)


def spread(wide, c, first, n, values):
    for h in range(2):
        wide[h, pl.ds(first * SUB + c, n, stride=SUB), :] = values[:, h * 128 : (h + 1) * 128]


def gather(wide, c, n):
    return jnp.concatenate([wide[h, pl.ds(c, n, stride=SUB), :] for h in range(2)], axis=1)


def chunk(c):
    return pl.ds(pl.multiple_of(c * LANE, LANE), LANE)


def compact_kernel(
    x_ref, dest_hbm, lab_ref, out_ref, ok_ref,
    dest_ref, xv, hat, wide, send_r, send_s, land_s, own, beside, rows, out_r, out_s, back_s, cand, ret_r, ret_s,
    mark, marks, counts, place, pick, unpick, sides, lives, choice, weights, scores,
    in_sem, lab_send, lab_recv,
    r_send, r_recv, s_send, s_recv, m_send, m_recv, yr_send, yr_recv, ys_send, ys_recv,
    rb_send, rb_recv, mb_send, mb_recv, sb_send, sb_recv,
):
    group = lax.axis_index("group")
    pair = lax.axis_index("pair")
    z, x = group // XS, group % XS

    def at(zz, xx):
        return (zz * XS + xx, pair)

    def z_peer(t):
        return lax.rem(z + distance_at(t), ZS)

    def x_peer(j):
        return lax.rem(x + j, XS)

    def pair_peer(side):
        return lax.rem(pair + jnp.where(side == 0, 1, PAIRS - 1), PAIRS)

    def remote(source, target, send, recv, device):
        return pltpu.make_async_remote_copy(
            source, target, send, recv, device_id=device, device_id_type=MESH
        )

    load_x = pltpu.make_async_copy(x_ref, xv, in_sem.at[0])
    load_dest = pltpu.make_async_copy(dest_hbm, dest_ref, in_sem.at[1])
    load_dest.start()
    load_x.start()
    barrier = pltpu.get_barrier_semaphore()

    @pl.loop(1, GROUPS)
    def _(d):
        pl.semaphore_signal(
            barrier, inc=1, device_id=(lax.rem(group + d, GROUPS), pair), device_id_type=MESH
        )

    for step in (1, PAIRS - 1):
        pl.semaphore_signal(
            barrier, inc=1, device_id=(group, lax.rem(pair + step, PAIRS)), device_id_type=MESH
        )

    load_dest.wait()
    turned = dest_ref[...].T
    for parity in range(2):
        part = turned[parity * COUNT : (parity + 1) * COUNT, :]
        unit = jnp.left_shift(jnp.ones_like(part), (part & 7) * 4)
        for k in range(GROUPS // 8):
            held = jnp.sum(jnp.where((part >> 3) == k, unit, 0), axis=0, keepdims=True)
            nibble = jnp.broadcast_to(held, (8, 256)) >> (iota((8, 256), 0) * 4)
            counts[parity, 8 * k : 8 * k + 8, :] = (nibble & 3).astype(f32)
    second = [(counts[parity] == 2.0).astype(f32) for parity in range(2)]
    both = (second[0] + second[1]).astype(bf16)
    need_col = jnp.sum(second[0] + second[1], axis=1, keepdims=True)
    need_row = lax.dot_general(
        jnp.ones((8, 256), bf16), both, along_rows, preferred_element_type=f32
    )[0:1, :]
    g_col, g_row = iota((GROUPS, GROUPS), 0), iota((GROUPS, GROUPS), 1)
    ahead = jnp.logical_or(
        need_row > need_col, jnp.logical_and(need_row == need_col, g_row < g_col)
    )
    standing = jnp.sum(ahead.astype(i32), axis=1, keepdims=True)
    position = (standing % ZS) * XS + standing // ZS
    place[...] = jnp.broadcast_to(position, (GROUPS, 128))

    cell = group * (PAIRS // 2) + pair // 2
    line = dest_ref[pl.ds(cell, 1), :]
    lane = iota((1, 128), 1)
    mine = lane // COUNT == pair % 2
    line = jnp.where(mine, line, -1)
    eye = iota((128, 128), 0) == iota((128, 128), 1)
    line_col = jnp.sum(jnp.where(eye, jnp.broadcast_to(line, (128, 128)), 0), axis=1, keepdims=True)
    earlier = jnp.logical_and(line_col == line, iota((128, 128), 0) < iota((128, 128), 1))
    rank = jnp.sum(earlier.astype(i32), axis=0, keepdims=True)
    spot = jnp.sum(
        jnp.where(iota((GROUPS, 128), 0) == line, place[...], 0), axis=0, keepdims=True
    )
    step = step_of((spot // XS - z + ZS) % ZS)
    slot = jnp.where(rank == 0, step * XS + spot % XS, GROUPS + step)
    slot = jnp.where(mine, slot, -1)
    fold = slot[:, :COUNT] + slot[:, COUNT:] + 1
    slot_col = jnp.sum(
        jnp.where(
            iota((COUNT, COUNT), 0) == iota((COUNT, COUNT), 1),
            jnp.broadcast_to(fold, (COUNT, COUNT)),
            0,
        ),
        axis=1,
        keepdims=True,
    )
    pick[...] = (iota((SENT, COUNT), 0) == fold).astype(f32).astype(bf16)
    unpick[...] = (iota((COUNT, SENT), 1) == slot_col).astype(f32).astype(bf16)
    mark[...] = jnp.zeros((1, 128), i32)
    mark[:, 0:PAIRS] = lab_ref[...]
    marks[pl.ds(group, 1), :, :] = mark[...].reshape(1, 1, 128)

    load_x.wait()

    @pl.loop(0, COUNT // 16)
    def _(i):
        r = pl.ds(pl.multiple_of(i * 16, 16), 16)
        values = xv[r, :].astype(f32)
        factor = lax.rsqrt(jnp.mean(values * values, axis=-1, keepdims=True) + 1e-05)
        hat[r, :] = (values * factor * (1.0 / math.sqrt(WIDTH))).astype(bf16)

    @pl.loop(0, SUB, unroll=UNROLL)
    def _(c):
        got = jnp.dot(pick[...], hat[:, chunk(c)], preferred_element_type=f32)
        spread(wide, c, 0, SENT, got)

    send_s[...] = docs_of(wide, GROUPS, ZS)

    def lab_x(j):
        here = marks.at[pl.ds(group, 1)]
        return remote(here, here, lab_send.at[0], lab_recv.at[0], at(z, x_peer(j)))

    def lab_z(t):
        here = marks.at[pl.ds(z * XS, XS)]
        return remote(here, here, lab_send.at[1], lab_recv.at[1], at(z_peer(t), x))

    def r_out(t, j):
        to = x_peer(j)
        return remote(
            send_r.at[t * XS + to], own.at[0, mirror(t), x], r_send, r_recv.at[t // BATCH],
            at(z_peer(t), to),
        )

    def s_out(t):
        return remote(send_s.at[t], land_s.at[mirror(t)], s_send, s_recv.at[t // QUAD], at(z_peer(t), x))

    def s_share(k, j):
        four = pl.ds(k * QUAD, QUAD)
        return remote(land_s.at[four], own.at[1, four, x], m_send, m_recv.at[k], at(z, x_peer(j)))

    def yr_out(b, side):
        two = pl.ds(b * BATCH, BATCH)
        return remote(
            own.at[0, two], beside.at[side, 0, two], yr_send, yr_recv.at[b],
            (group, pair_peer(side)),
        )

    def ys_out(k, side):
        four = pl.ds(k * QUAD, QUAD)
        return remote(
            own.at[1, four], beside.at[side, 1, four], ys_send, ys_recv.at[k],
            (group, pair_peer(side)),
        )

    def r_batch(b, act):
        for k in range(BATCH):
            t = b * BATCH + k
            for j in range(XS):
                if j == 0 and k == 0:
                    @pl.when(t > 0)
                    def _():
                        act(t, j)
                else:
                    act(t, j)

    def local(source, target, sem):
        pltpu.make_async_copy(source, target, sem).start()

    def settle(arrived, sem):
        pltpu.make_async_copy(arrived, arrived, sem).wait()

    pl.semaphore_wait(barrier, GROUPS - 1 + 2)

    for j in range(1, XS):
        lab_x(j).start()

    @pl.loop(1, ZS)
    def _(t):
        s_out(t).start()

    local(send_s.at[0], land_s.at[0], s_recv.at[0])

    @pl.loop(0, BATCHES)
    def _(b):
        send_r[pl.ds(b * BATCH * XS, BATCH * XS)] = docs_of(wide, b * BATCH * XS, BATCH * XS)

        @pl.when(b < AHEAD)
        def _():
            r_batch(b, lambda t, j: r_out(t, j).start())

    local(send_r.at[x], own.at[0, 0, x], r_recv.at[0])
    settle(marks.at[pl.ds(0, XS - 1)], lab_recv.at[0])

    @pl.loop(1, ZS)
    def _(t):
        lab_z(t).start()

    @pl.loop(0, QUADS)
    def _(k):
        four = pl.ds(k * QUAD, QUAD)
        settle(land_s.at[four], s_recv.at[k])
        for j in range(1, XS):
            s_share(k, j).start()
        local(land_s.at[four], own.at[1, four, x], m_recv.at[k])

    here = place[:, 0:1] == group
    held = [
        jnp.sum(jnp.where(here, counts[parity], 0.0), axis=0, keepdims=True) for parity in range(2)
    ]
    s_lane = iota((256, BLOCK), 1)
    s_source = lax.rem(z + distance_at((s_lane // XS) % ZS), ZS) * XS + s_lane % XS
    for n, shift in enumerate((0, PAIRS - 1, 1)):
        other = lax.rem(pair + shift, PAIRS)
        row = jnp.where(other % 2 == 0, held[0], held[1])
        chosen = (iota((256, BLOCK), 0) == s_source * (PAIRS // 2) + other // 2).astype(f32)
        filled = jnp.dot(
            jnp.broadcast_to(row, (8, 256)).astype(bf16), chosen.astype(bf16),
            preferred_element_type=f32,
        )
        lives[n] = (filled > (iota((8, BLOCK), 1) // GROUPS).astype(f32)).astype(f32)

    at_here = (place[:, 0:GROUPS] == z * XS + iota((GROUPS, GROUPS), 1) % XS).astype(f32)
    wanted = jnp.where(
        pair % 2 == 0, (counts[0] == 2.0).astype(f32), (counts[1] == 2.0).astype(f32)
    )
    owner_of = lax.dot_general(
        at_here.astype(bf16), wanted.astype(bf16), along_cols, preferred_element_type=f32
    )
    t_row = iota((GROUPS, 256), 0) // XS
    c_row = (lax.rem(z + distance_at(t_row), ZS) * XS + x) * (PAIRS // 2) + pair // 2
    choice[...] = jnp.broadcast_to(
        jnp.sum(jnp.where(iota((GROUPS, 256), 1) == c_row, owner_of, 0.0), axis=1, keepdims=True),
        (GROUPS, 128),
    )

    plane = (place[:, 0:ZS] // XS == iota((GROUPS, ZS), 1)).astype(f32).astype(bf16)
    most = jnp.zeros((1, 1), f32)
    for parity in range(2):
        load = lax.dot_general(
            plane, (counts[parity] == 2.0).astype(f32).astype(bf16), along_cols,
            preferred_element_type=f32,
        )
        most = jnp.maximum(most, jnp.max(jnp.max(load, axis=1, keepdims=True), axis=0, keepdims=True))
    ok_ref[...] = (most < 1.5).astype(i32)

    def read_labels():
        settle(marks.at[pl.ds(0, GROUPS - XS)], lab_recv.at[1])

        def add_marks(g, total):
            return total + jnp.where(place[pl.ds(g, 1), :] == group, marks[g], 0)

        label = lax.fori_loop(0, GROUPS, add_marks, jnp.zeros((1, 128), i32))

        def label_at(q):
            return jnp.sum(jnp.where(lane == q, label, 0), axis=1, keepdims=True)

        joined_prev = jnp.logical_and(label_at(pair - 1) == label_at(pair), pair > 0)
        joined_next = jnp.logical_and(label_at(pair + 1) == label_at(pair), pair < PAIRS - 1)
        sides[0] = jnp.broadcast_to(joined_prev.astype(f32), (8, 128))
        sides[1] = jnp.broadcast_to(joined_next.astype(f32), (8, 128))

    def to_rows(first):
        @pl.loop(0, SUB, unroll=UNROLL)
        def _(c):
            rows[c, pl.ds(pl.multiple_of(first, 16), 16), :] = gather(wide, c, 16).astype(bf16)

    def own_rows(kind, k):
        put_wide(wide, 0, own[kind, pl.ds(k * QUAD, QUAD)].reshape(16, SUB, LANE))
        to_rows(kind * GROUPS + k * 16)

    def beside_rows(kind, k):
        four = pl.ds(k * QUAD, QUAD)
        flag = sides[0][0:1, :]
        flag = jnp.broadcast_to(jnp.concatenate([flag, flag], axis=1), (16 * SUB, LANE))
        prev = beside[0, kind, four].reshape(16 * SUB, LANE).astype(f32)
        nxt = beside[1, kind, four].reshape(16 * SUB, LANE).astype(f32)
        put_wide(wide, 0, jnp.where(flag > 0.5, prev, nxt).reshape(16, SUB, LANE))
        to_rows(BLOCK + kind * GROUPS + k * 16)

    def beside_r(k):
        for i in range(2):
            two = pl.ds((2 * k + i) * BATCH, BATCH)
            settle(beside.at[:, 0, two], yr_recv.at[2 * k + i])
        beside_rows(0, k)

    @pl.loop(0, QUADS)
    def _(k):
        settle(own.at[1, pl.ds(k * QUAD, QUAD)], m_recv.at[k])
        for side in range(2):
            ys_out(k, side).start()

    @pl.loop(0, BATCHES)
    def _(b):
        settle(own.at[0, pl.ds(b * BATCH, BATCH)], r_recv.at[b])

        @pl.when(b + AHEAD < BATCHES)
        def _():
            r_batch(b + AHEAD, lambda t, j: r_out(t, j).start())

        for side in range(2):
            yr_out(b, side).start()

        @pl.when(b % 2 == 1)
        def _():
            own_rows(0, b // 2)
            own_rows(1, b // 2)

        pl.when(b == 3)(read_labels)

        @pl.when(b >= 4)
        def _():
            k = b - 4
            settle(beside.at[:, 1, pl.ds(k * QUAD, QUAD)], ys_recv.at[k])
            beside_rows(1, k)

            @pl.when(k >= 2)
            def _():
                beside_r(k - 2)

    def add_own(c, total):
        mine = rows[c, 0:BLOCK]
        return total + lax.dot_general(mine, mine, along_rows, preferred_element_type=f32)

    scores[:, 0:BLOCK] = lax.fori_loop(
        0, SUB, add_own, jnp.zeros((BLOCK, BLOCK), f32), unroll=UNROLL
    )

    @pl.loop(2, QUADS)
    def _(k):
        beside_r(k)

    prev_mask = lives[1][0:1, :] * sides[0][0:1, :]
    next_mask = lives[2][0:1, :] * sides[1][0:1, :]
    side_mask = jnp.broadcast_to(prev_mask + next_mask, (GROUPS, BLOCK))

    def smooth(kind):
        part = pl.ds(kind * GROUPS, GROUPS)

        def add_side(c, total):
            return total + lax.dot_general(
                rows[c, part], rows[c, BLOCK : 2 * BLOCK], along_rows, preferred_element_type=f32
            )

        scores[part, BLOCK : 2 * BLOCK] = lax.fori_loop(
            0, SUB, add_side, jnp.zeros((GROUPS, BLOCK), f32), unroll=UNROLL
        )
        apart = (iota((GROUPS, BLOCK), 0) + kind * GROUPS != iota((GROUPS, BLOCK), 1)).astype(f32)
        mask = jnp.concatenate([lives[0][0:1, :] * apart, side_mask], axis=1)
        raw = jnp.exp(score_scale * scores[part, :]) * mask
        weights[...] = raw.astype(bf16)
        denom = self_weight + jnp.sum(raw, axis=1, keepdims=True)
        scale = jnp.broadcast_to(math.sqrt(WIDTH) / denom, (GROUPS, LANE))

        @pl.loop(0, SUB, unroll=UNROLL)
        def _(c):
            numer = self_weight * rows[c, part].astype(f32) + jnp.dot(
                weights[...], rows[c], preferred_element_type=f32
            )
            spread(wide, c, kind * GROUPS, GROUPS, numer * scale)

    def r_home(t, j):
        to = x_peer(j)
        return remote(
            out_r.at[t * XS + to], ret_r.at[mirror(t), x], rb_send, rb_recv.at[t // BATCH],
            at(z_peer(t), to),
        )

    def s_back(k, j):
        four, to = pl.ds(k * QUAD, QUAD), x_peer(j)
        return remote(out_s.at[four, to], cand.at[four, x], mb_send, mb_recv.at[k], at(z, to))

    def s_home(t):
        return remote(back_s.at[t], ret_s.at[mirror(t)], sb_send, sb_recv, at(z_peer(t), x))

    smooth(0)

    @pl.loop(0, BATCHES)
    def _(b):
        out_r[pl.ds(b * BATCH * XS, BATCH * XS)] = docs_of(wide, b * BATCH * XS, BATCH * XS)

        @pl.when(b < FIRST)
        def _():
            r_batch(b, lambda t, j: r_home(t, j).start())

    local(out_r.at[x], ret_r.at[0, x], rb_recv.at[0])

    smooth(1)

    @pl.loop(0, QUADS)
    def _(k):
        four = pl.ds(k * QUAD, QUAD)
        out_s[four] = docs_of(wide, GROUPS + k * 16, 16).reshape(QUAD, XS, SUB, LANE)
        for j in range(1, XS):
            s_back(k, j).start()
        local(out_s.at[four, x], cand.at[four, x], mb_recv.at[k])

    def choose(t):
        chosen = cand[t, XS - 1].astype(f32)
        for k in range(XS - 1):
            flag = choice[pl.ds(t * XS + k, 1), :]
            flag = jnp.broadcast_to(jnp.concatenate([flag, flag], axis=1), (SUB, LANE))
            chosen = jnp.where(flag > 0.5, cand[t, k].astype(f32), chosen)
        back_s[t] = chosen.astype(bf16)

    @pl.loop(0, QUADS)
    def _(k):
        settle(cand.at[pl.ds(k * QUAD, QUAD)], mb_recv.at[k])
        for i in range(QUAD):
            t = k * QUAD + i
            choose(t)
            if i == 0:
                @pl.when(t > 0)
                def _():
                    s_home(t).start()
            else:
                s_home(t).start()

    @pl.loop(FIRST, BATCHES)
    def _(b):
        r_batch(b, lambda t, j: r_home(t, j).start())

    local(back_s.at[0], ret_s.at[0], sb_recv)

    @pl.loop(0, BATCHES)
    def _(b):
        two = pl.ds(b * BATCH, BATCH)
        settle(ret_r.at[two], rb_recv.at[b])
        put_wide(wide, b * BATCH * XS, ret_r[two].reshape(BATCH * XS, SUB, LANE))

    settle(ret_s, sb_recv)
    put_wide(wide, GROUPS, ret_s[...])

    @pl.loop(0, SUB, unroll=UNROLL)
    def _(c):
        got = gather(wide, c, SENT).astype(bf16)
        out_ref[:, chunk(c)] = jnp.dot(unpick[...], got, preferred_element_type=f32).astype(bf16)

    settle(marks.at[pl.ds(0, XS - 1)], lab_send.at[0])
    settle(marks.at[pl.ds(0, GROUPS - XS)], lab_send.at[1])
    settle(send_r.at[pl.ds(0, GROUPS - 1)], r_send)
    settle(send_s.at[pl.ds(0, ZS - 1)], s_send)
    settle(send_r.at[pl.ds(0, GROUPS - ZS)], m_send)
    settle(own, yr_send)
    settle(own, ys_send)
    settle(out_r.at[pl.ds(0, GROUPS - 1)], rb_send)
    settle(out_r.at[pl.ds(0, GROUPS - ZS)], mb_send)
    settle(back_s.at[pl.ds(0, ZS - 1)], sb_send)


def compact(embeddings, dest, labels):
    vmem = pl.BlockSpec(memory_space=pltpu.VMEM)
    dma = pltpu.SemaphoreType.DMA
    return pl.pallas_call(
        compact_kernel,
        out_shape=(
            jax.ShapeDtypeStruct((COUNT, WIDTH), bf16),
            jax.ShapeDtypeStruct((1, 1), i32),
        ),
        in_specs=[pl.BlockSpec(memory_space=pl.ANY)] * 2 + [vmem],
        out_specs=(vmem, vmem),
        scratch_shapes=[
            pltpu.VMEM((256, 128), i32),
            pltpu.VMEM((COUNT, WIDTH), bf16),
            pltpu.VMEM((COUNT, WIDTH), bf16),
            pltpu.VMEM((2, BLOCK * SUB, 128), f32),
            pltpu.VMEM((GROUPS, SUB, LANE), bf16),
            pltpu.VMEM((ZS, SUB, LANE), bf16),
            pltpu.VMEM((ZS, SUB, LANE), bf16),
            pltpu.VMEM((2, ZS, XS, SUB, LANE), bf16),
            pltpu.VMEM((2, 2, ZS, XS, SUB, LANE), bf16),
            pltpu.VMEM((SUB, 2 * BLOCK, LANE), bf16),
            pltpu.VMEM((GROUPS, SUB, LANE), bf16),
            pltpu.VMEM((ZS, XS, SUB, LANE), bf16),
            pltpu.VMEM((ZS, SUB, LANE), bf16),
            pltpu.VMEM((ZS, XS, SUB, LANE), bf16),
            pltpu.VMEM((ZS, XS, SUB, LANE), bf16),
            pltpu.VMEM((ZS, SUB, LANE), bf16),
            pltpu.VMEM((1, 128), i32),
            pltpu.VMEM((GROUPS, 1, 128), i32),
            pltpu.VMEM((2, GROUPS, 256), f32),
            pltpu.VMEM((GROUPS, 128), i32),
            pltpu.VMEM((SENT, COUNT), bf16),
            pltpu.VMEM((COUNT, SENT), bf16),
            pltpu.VMEM((2, 8, 128), f32),
            pltpu.VMEM((3, 8, BLOCK), f32),
            pltpu.VMEM((GROUPS, 128), f32),
            pltpu.VMEM((GROUPS, 2 * BLOCK), bf16),
            pltpu.VMEM((BLOCK, 2 * BLOCK), f32),
            dma((2,)), dma((2,)), dma((2,)),
            dma(()), dma((BATCHES,)), dma(()), dma((QUADS,)), dma(()), dma((QUADS,)),
            dma(()), dma((BATCHES,)), dma(()), dma((QUADS,)),
            dma(()), dma((BATCHES,)), dma(()), dma((QUADS,)), dma(()), dma(()),
        ],
        compiler_params=pltpu.CompilerParams(
            collective_id=0, has_side_effects=True, vmem_limit_bytes=40 << 20
        ),
    )(embeddings, dest, labels)


def on_device(embeddings, dest, labels):
    out, ok = compact(embeddings, dest.reshape(GROUPS * PAIRS * COUNT // 128, 128), labels)
    return lax.cond(ok.reshape(()) == 1, lambda: out, lambda: padded(embeddings, dest, labels))


def solution(mesh):
    in_specs = (P(("group", "pair"), None), P(), P("group", None))
    out_specs = P(("group", "pair"), None)
    return jax.shard_map(
        on_device, mesh=mesh, in_specs=in_specs, out_specs=out_specs, check_vma=False
    )
```

```python
import math

import jax
import jax.numpy as jnp
from jax import lax
from jax.experimental import pallas as pl
from jax.experimental.pallas import tpu as pltpu
from jax.sharding import PartitionSpec as P

score_scale = 64.0
self_weight = math.exp(4.0)
along_rows = (((1,), (1,)), ((), ()))
along_cols = (((0,), (0,)), ((), ()))


def shifted(block, axis, distance):
    devices = range(lax.axis_size(axis))
    route = [(i - distance, i) for i in devices if i - distance in devices]
    return lax.ppermute(block, axis, route)


def normalized(rows):
    values = rows.astype(jnp.float32)
    factor = lax.rsqrt(jnp.mean(values * values, axis=-1, keepdims=True) + 1e-05)
    return (values * factor * (1.0 / math.sqrt(values.shape[-1]))).astype(jnp.bfloat16)


def live_slots(routes, source_pair, owner, capacity):
    column = lax.dynamic_index_in_dim(routes, source_pair, axis=1, keepdims=False)
    counts = jnp.sum((column == owner).astype(jnp.int32), axis=1)
    return (
        (jnp.arange(capacity, dtype=jnp.int32)[None, :] < counts[:, None])
        .reshape(-1)
        .astype(jnp.float32)
    )


def pair_weights(left, right, mask):
    scores = lax.dot_general(left, right, along_rows, preferred_element_type=jnp.float32)
    return jnp.exp(score_scale * scores) * mask


def padded(embeddings, dest, labels):
    groups = lax.axis_size("group")
    pairs = lax.axis_size("pair")
    group_at = lax.axis_index("group")
    pair_at = lax.axis_index("pair")
    count = embeddings.shape[0]
    width = embeddings.shape[1]
    capacity = 2 * count // groups
    slots = groups * capacity
    routes = dest.reshape(groups, pairs, count)
    own_routes = lax.dynamic_index_in_dim(
        lax.dynamic_index_in_dim(routes, group_at, axis=0, keepdims=False),
        pair_at,
        axis=0,
        keepdims=False,
    )
    hits = (own_routes[:, None] == jnp.arange(groups, dtype=jnp.int32)[None, :]).astype(jnp.int32)
    ranks = jnp.sum(jnp.cumsum(hits, axis=0) * hits, axis=1) - 1
    slot = own_routes * capacity + ranks
    match = (slot[None, :] == jnp.arange(slots, dtype=jnp.int32)[:, None]).astype(jnp.int32)
    slot_doc = jnp.sum(match * jnp.arange(count, dtype=jnp.int32)[None, :], axis=1)
    filled = jnp.sum(match, axis=1)
    hat = normalized(embeddings)
    outgoing = jnp.where(filled[:, None] > 0, hat[slot_doc], jnp.zeros((), jnp.bfloat16))
    arrived = lax.all_to_all(
        outgoing.reshape(groups, capacity, width), "group", split_axis=0, concat_axis=0, tiled=True
    )
    block = arrived.reshape(slots, width)
    marks = labels[0]
    mine = marks[pair_at]
    live_mine = live_slots(routes, pair_at, group_at, capacity)
    next_at = jnp.minimum(pair_at + 1, pairs - 1)
    joined_next = jnp.logical_and(pair_at + 1 < pairs, marks[next_at] == mine).astype(jnp.float32)
    live_next = live_slots(routes, next_at, group_at, capacity)
    apart = (jnp.arange(slots)[:, None] != jnp.arange(slots)[None, :]).astype(jnp.float32)
    own_weights = pair_weights(block, block, live_mine[None, :] * apart)
    numer = self_weight * block.astype(jnp.float32) + jnp.dot(
        own_weights.astype(jnp.bfloat16), block, preferred_element_type=jnp.float32
    )
    denom = self_weight + jnp.sum(own_weights, axis=1)
    neighbour = shifted(block, "pair", -1)
    next_weights = pair_weights(
        block, neighbour, live_mine[:, None] * live_next[None, :] * joined_next
    )
    next_rounded = next_weights.astype(jnp.bfloat16)
    numer = numer + jnp.dot(next_rounded, neighbour, preferred_element_type=jnp.float32)
    denom = denom + jnp.sum(next_weights, axis=1)
    column_numer = lax.dot_general(
        next_rounded, block, along_cols, preferred_element_type=jnp.float32
    )
    column_denom = jnp.sum(next_weights, axis=0)
    came_numer, came_denom = (
        shifted(column_numer.astype(jnp.bfloat16), "pair", 1).astype(column_numer.dtype),
        shifted(column_denom.astype(jnp.bfloat16), "pair", 1).astype(column_denom.dtype),
    )
    numer = numer + came_numer
    denom = denom + came_denom
    block_out = (math.sqrt(width) * numer / denom[:, None]).astype(jnp.bfloat16)
    returned = lax.all_to_all(
        block_out.reshape(groups, capacity, width), "group", split_axis=0, concat_axis=0, tiled=True
    )
    return returned.reshape(slots, width)[slot]


ZS, XS, PAIRS, COUNT, WIDTH = 16, 4, 8, 64, 4096
GROUPS = ZS * XS
SUB, LANE = 16, 256
BLOCK = GROUPS * 2
SENT = GROUPS + ZS
BATCH = 2
BATCHES = ZS // BATCH
QUAD = 4
QUADS = ZS // QUAD
AHEAD = 5
UNROLL = 16
FIRST = 4
MESH = pl.DeviceIdType.MESH
f32, bf16, i32 = jnp.float32, jnp.bfloat16, jnp.int32


def distance_at(t):
    half = t // 2
    far = jnp.where(t % 2 == 0, 8 - half, 8 + half)
    return jnp.where(t == 0, 0, far)


def step_of(distance):
    near = jnp.where(distance < 8, 16 - 2 * distance, 2 * distance - 15)
    return jnp.where(distance == 0, 0, near)


def mirror(t):
    return jnp.where(t < 2, t, jnp.where(t % 2 == 0, t + 1, t - 1))


def iota(shape, axis):
    return lax.broadcasted_iota(i32, shape, axis)


def put_wide(wide, first, docs):
    n = docs.shape[0]
    flat = docs.astype(f32).reshape(n * SUB, LANE)
    for h in range(2):
        wide[h, pl.ds(pl.multiple_of(first * SUB, SUB), n * SUB), :] = flat[:, h * 128 : (h + 1) * 128]


def docs_of(wide, first, n):
    at = pl.ds(pl.multiple_of(first * SUB, SUB), n * SUB)
    flat = jnp.concatenate([wide[0, at, :], wide[1, at, :]], axis=1)
    return flat.astype(bf16).reshape(n, SUB, LANE)


def spread(wide, c, first, n, values):
    for h in range(2):
        wide[h, pl.ds(first * SUB + c, n, stride=SUB), :] = values[:, h * 128 : (h + 1) * 128]


def gather(wide, c, n):
    return jnp.concatenate([wide[h, pl.ds(c, n, stride=SUB), :] for h in range(2)], axis=1)


def chunk(c):
    return pl.ds(pl.multiple_of(c * LANE, LANE), LANE)


def compact_kernel(
    x_ref, dest_hbm, lab_ref, out_ref, ok_ref,
    dest_ref, xv, hat, wide, send_r, send_s, land_s, own, beside, rows, out_r, out_s, back_s, cand, ret_r, ret_s,
    mark, marks, counts, place, pick, unpick, sides, lives, choice, weights, scores,
    in_sem, lab_send, lab_recv,
    r_send, r_recv, s_send, s_recv, m_send, m_recv, yr_send, yr_recv, ys_send, ys_recv,
    rb_send, rb_recv, mb_send, mb_recv, sb_send, sb_recv,
):
    group = lax.axis_index("group")
    pair = lax.axis_index("pair")
    z, x = group // XS, group % XS

    def at(zz, xx):
        return (zz * XS + xx, pair)

    def z_peer(t):
        return lax.rem(z + distance_at(t), ZS)

    def x_peer(j):
        return lax.rem(x + j, XS)

    def pair_peer(side):
        return lax.rem(pair + jnp.where(side == 0, 1, PAIRS - 1), PAIRS)

    def remote(source, target, send, recv, device):
        return pltpu.make_async_remote_copy(
            source, target, send, recv, device_id=device, device_id_type=MESH
        )

    load_x = pltpu.make_async_copy(x_ref, xv, in_sem.at[0])
    load_dest = pltpu.make_async_copy(dest_hbm, dest_ref, in_sem.at[1])
    load_dest.start()
    load_x.start()
    barrier = pltpu.get_barrier_semaphore()

    @pl.loop(1, GROUPS)
    def _(d):
        pl.semaphore_signal(
            barrier, inc=1, device_id=(lax.rem(group + d, GROUPS), pair), device_id_type=MESH
        )

    for step in (1, PAIRS - 1):
        pl.semaphore_signal(
            barrier, inc=1, device_id=(group, lax.rem(pair + step, PAIRS)), device_id_type=MESH
        )

    load_dest.wait()
    turned = dest_ref[...].T
    for parity in range(2):
        part = turned[parity * COUNT : (parity + 1) * COUNT, :]
        unit = jnp.left_shift(jnp.ones_like(part), (part & 7) * 4)
        for k in range(GROUPS // 8):
            held = jnp.sum(jnp.where((part >> 3) == k, unit, 0), axis=0, keepdims=True)
            nibble = jnp.broadcast_to(held, (8, 256)) >> (iota((8, 256), 0) * 4)
            counts[parity, 8 * k : 8 * k + 8, :] = (nibble & 3).astype(f32)
    second = [(counts[parity] == 2.0).astype(f32) for parity in range(2)]
    both = (second[0] + second[1]).astype(bf16)
    need_col = jnp.sum(second[0] + second[1], axis=1, keepdims=True)
    need_row = lax.dot_general(
        jnp.ones((8, 256), bf16), both, along_rows, preferred_element_type=f32
    )[0:1, :]
    g_col, g_row = iota((GROUPS, GROUPS), 0), iota((GROUPS, GROUPS), 1)
    ahead = jnp.logical_or(
        need_row > need_col, jnp.logical_and(need_row == need_col, g_row < g_col)
    )
    standing = jnp.sum(ahead.astype(i32), axis=1, keepdims=True)
    position = (standing % ZS) * XS + standing // ZS
    place[...] = jnp.broadcast_to(position, (GROUPS, 128))

    cell = group * (PAIRS // 2) + pair // 2
    line = dest_ref[pl.ds(cell, 1), :]
    lane = iota((1, 128), 1)
    mine = lane // COUNT == pair % 2
    line = jnp.where(mine, line, -1)
    eye = iota((128, 128), 0) == iota((128, 128), 1)
    line_col = jnp.sum(jnp.where(eye, jnp.broadcast_to(line, (128, 128)), 0), axis=1, keepdims=True)
    earlier = jnp.logical_and(line_col == line, iota((128, 128), 0) < iota((128, 128), 1))
    rank = jnp.sum(earlier.astype(i32), axis=0, keepdims=True)
    spot = jnp.sum(
        jnp.where(iota((GROUPS, 128), 0) == line, place[...], 0), axis=0, keepdims=True
    )
    step = step_of((spot // XS - z + ZS) % ZS)
    slot = jnp.where(rank == 0, step * XS + spot % XS, GROUPS + step)
    slot = jnp.where(mine, slot, -1)
    fold = slot[:, :COUNT] + slot[:, COUNT:] + 1
    slot_col = jnp.sum(
        jnp.where(
            iota((COUNT, COUNT), 0) == iota((COUNT, COUNT), 1),
            jnp.broadcast_to(fold, (COUNT, COUNT)),
            0,
        ),
        axis=1,
        keepdims=True,
    )
    pick[...] = (iota((SENT, COUNT), 0) == fold).astype(f32).astype(bf16)
    unpick[...] = (iota((COUNT, SENT), 1) == slot_col).astype(f32).astype(bf16)
    mark[...] = jnp.zeros((1, 128), i32)
    mark[:, 0:PAIRS] = lab_ref[...]
    marks[pl.ds(group, 1), :, :] = mark[...].reshape(1, 1, 128)

    load_x.wait()

    @pl.loop(0, COUNT // 16)
    def _(i):
        r = pl.ds(pl.multiple_of(i * 16, 16), 16)
        values = xv[r, :].astype(f32)
        factor = lax.rsqrt(jnp.mean(values * values, axis=-1, keepdims=True) + 1e-05)
        hat[r, :] = (values * factor * (1.0 / math.sqrt(WIDTH))).astype(bf16)

    @pl.loop(0, SUB, unroll=UNROLL)
    def _(c):
        got = jnp.dot(pick[...], hat[:, chunk(c)], preferred_element_type=f32)
        spread(wide, c, 0, SENT, got)

    send_s[...] = docs_of(wide, GROUPS, ZS)

    def lab_x(j):
        here = marks.at[pl.ds(group, 1)]
        return remote(here, here, lab_send.at[0], lab_recv.at[0], at(z, x_peer(j)))

    def lab_z(t):
        here = marks.at[pl.ds(z * XS, XS)]
        return remote(here, here, lab_send.at[1], lab_recv.at[1], at(z_peer(t), x))

    def r_out(t, j):
        to = x_peer(j)
        return remote(
            send_r.at[t * XS + to], own.at[0, mirror(t), x], r_send, r_recv.at[t // BATCH],
            at(z_peer(t), to),
        )

    def s_out(t):
        return remote(send_s.at[t], land_s.at[mirror(t)], s_send, s_recv.at[t // QUAD], at(z_peer(t), x))

    def s_share(k, j):
        four = pl.ds(k * QUAD, QUAD)
        return remote(land_s.at[four], own.at[1, four, x], m_send, m_recv.at[k], at(z, x_peer(j)))

    def yr_out(b, side):
        two = pl.ds(b * BATCH, BATCH)
        return remote(
            own.at[0, two], beside.at[side, 0, two], yr_send, yr_recv.at[b],
            (group, pair_peer(side)),
        )

    def ys_out(k, side):
        four = pl.ds(k * QUAD, QUAD)
        return remote(
            own.at[1, four], beside.at[side, 1, four], ys_send, ys_recv.at[k],
            (group, pair_peer(side)),
        )

    def r_batch(b, act):
        for k in range(BATCH):
            t = b * BATCH + k
            for j in range(XS):
                if j == 0 and k == 0:
                    @pl.when(t > 0)
                    def _():
                        act(t, j)
                else:
                    act(t, j)

    def local(source, target, sem):
        pltpu.make_async_copy(source, target, sem).start()

    def settle(arrived, sem):
        pltpu.make_async_copy(arrived, arrived, sem).wait()

    pl.semaphore_wait(barrier, GROUPS - 1 + 2)

    for j in range(1, XS):
        lab_x(j).start()

    @pl.loop(1, ZS)
    def _(t):
        s_out(t).start()

    local(send_s.at[0], land_s.at[0], s_recv.at[0])

    @pl.loop(0, BATCHES)
    def _(b):
        send_r[pl.ds(b * BATCH * XS, BATCH * XS)] = docs_of(wide, b * BATCH * XS, BATCH * XS)

        @pl.when(b < AHEAD)
        def _():
            r_batch(b, lambda t, j: r_out(t, j).start())

    local(send_r.at[x], own.at[0, 0, x], r_recv.at[0])
    settle(marks.at[pl.ds(0, XS - 1)], lab_recv.at[0])

    @pl.loop(1, ZS)
    def _(t):
        lab_z(t).start()

    @pl.loop(0, QUADS)
    def _(k):
        four = pl.ds(k * QUAD, QUAD)
        settle(land_s.at[four], s_recv.at[k])
        for j in range(1, XS):
            s_share(k, j).start()
        local(land_s.at[four], own.at[1, four, x], m_recv.at[k])

    here = place[:, 0:1] == group
    held = [
        jnp.sum(jnp.where(here, counts[parity], 0.0), axis=0, keepdims=True) for parity in range(2)
    ]
    s_lane = iota((256, BLOCK), 1)
    s_source = lax.rem(z + distance_at((s_lane // XS) % ZS), ZS) * XS + s_lane % XS
    for n, shift in enumerate((0, PAIRS - 1, 1)):
        other = lax.rem(pair + shift, PAIRS)
        row = jnp.where(other % 2 == 0, held[0], held[1])
        chosen = (iota((256, BLOCK), 0) == s_source * (PAIRS // 2) + other // 2).astype(f32)
        filled = jnp.dot(
            jnp.broadcast_to(row, (8, 256)).astype(bf16), chosen.astype(bf16),
            preferred_element_type=f32,
        )
        lives[n] = (filled > (iota((8, BLOCK), 1) // GROUPS).astype(f32)).astype(f32)

    at_here = (place[:, 0:GROUPS] == z * XS + iota((GROUPS, GROUPS), 1) % XS).astype(f32)
    wanted = jnp.where(
        pair % 2 == 0, (counts[0] == 2.0).astype(f32), (counts[1] == 2.0).astype(f32)
    )
    owner_of = lax.dot_general(
        at_here.astype(bf16), wanted.astype(bf16), along_cols, preferred_element_type=f32
    )
    t_row = iota((GROUPS, 256), 0) // XS
    c_row = (lax.rem(z + distance_at(t_row), ZS) * XS + x) * (PAIRS // 2) + pair // 2
    choice[...] = jnp.broadcast_to(
        jnp.sum(jnp.where(iota((GROUPS, 256), 1) == c_row, owner_of, 0.0), axis=1, keepdims=True),
        (GROUPS, 128),
    )

    plane = (place[:, 0:ZS] // XS == iota((GROUPS, ZS), 1)).astype(f32).astype(bf16)
    most = jnp.zeros((1, 1), f32)
    for parity in range(2):
        load = lax.dot_general(
            plane, (counts[parity] == 2.0).astype(f32).astype(bf16), along_cols,
            preferred_element_type=f32,
        )
        most = jnp.maximum(most, jnp.max(jnp.max(load, axis=1, keepdims=True), axis=0, keepdims=True))
    ok_ref[...] = (most < 1.5).astype(i32)

    def read_labels():
        settle(marks.at[pl.ds(0, GROUPS - XS)], lab_recv.at[1])

        def add_marks(g, total):
            return total + jnp.where(place[pl.ds(g, 1), :] == group, marks[g], 0)

        label = lax.fori_loop(0, GROUPS, add_marks, jnp.zeros((1, 128), i32))

        def label_at(q):
            return jnp.sum(jnp.where(lane == q, label, 0), axis=1, keepdims=True)

        joined_prev = jnp.logical_and(label_at(pair - 1) == label_at(pair), pair > 0)
        joined_next = jnp.logical_and(label_at(pair + 1) == label_at(pair), pair < PAIRS - 1)
        sides[0] = jnp.broadcast_to(joined_prev.astype(f32), (8, 128))
        sides[1] = jnp.broadcast_to(joined_next.astype(f32), (8, 128))

    def to_rows(first):
        @pl.loop(0, SUB, unroll=UNROLL)
        def _(c):
            rows[c, pl.ds(pl.multiple_of(first, 16), 16), :] = gather(wide, c, 16).astype(bf16)

    def own_rows(kind, k):
        put_wide(wide, 0, own[kind, pl.ds(k * QUAD, QUAD)].reshape(16, SUB, LANE))
        to_rows(kind * GROUPS + k * 16)

    def beside_rows(kind, k):
        four = pl.ds(k * QUAD, QUAD)
        flag = sides[0][0:1, :]
        flag = jnp.broadcast_to(jnp.concatenate([flag, flag], axis=1), (16 * SUB, LANE))
        prev = beside[0, kind, four].reshape(16 * SUB, LANE).astype(f32)
        nxt = beside[1, kind, four].reshape(16 * SUB, LANE).astype(f32)
        put_wide(wide, 0, jnp.where(flag > 0.5, prev, nxt).reshape(16, SUB, LANE))
        to_rows(BLOCK + kind * GROUPS + k * 16)

    def beside_r(k):
        for i in range(2):
            two = pl.ds((2 * k + i) * BATCH, BATCH)
            settle(beside.at[:, 0, two], yr_recv.at[2 * k + i])
        beside_rows(0, k)

    @pl.loop(0, QUADS)
    def _(k):
        settle(own.at[1, pl.ds(k * QUAD, QUAD)], m_recv.at[k])
        for side in range(2):
            ys_out(k, side).start()

    @pl.loop(0, BATCHES)
    def _(b):
        settle(own.at[0, pl.ds(b * BATCH, BATCH)], r_recv.at[b])

        @pl.when(b + AHEAD < BATCHES)
        def _():
            r_batch(b + AHEAD, lambda t, j: r_out(t, j).start())

        for side in range(2):
            yr_out(b, side).start()

        @pl.when(b % 2 == 1)
        def _():
            own_rows(0, b // 2)
            own_rows(1, b // 2)

        pl.when(b == 3)(read_labels)

        @pl.when(b >= 4)
        def _():
            k = b - 4
            settle(beside.at[:, 1, pl.ds(k * QUAD, QUAD)], ys_recv.at[k])
            beside_rows(1, k)

            @pl.when(k >= 2)
            def _():
                beside_r(k - 2)

    def add_own(c, total):
        mine = rows[c, 0:BLOCK]
        return total + lax.dot_general(mine, mine, along_rows, preferred_element_type=f32)

    scores[:, 0:BLOCK] = lax.fori_loop(
        0, SUB, add_own, jnp.zeros((BLOCK, BLOCK), f32), unroll=UNROLL
    )

    @pl.loop(2, QUADS)
    def _(k):
        beside_r(k)

    prev_mask = lives[1][0:1, :] * sides[0][0:1, :]
    next_mask = lives[2][0:1, :] * sides[1][0:1, :]
    side_mask = jnp.broadcast_to(prev_mask + next_mask, (GROUPS, BLOCK))

    def smooth(kind):
        part = pl.ds(kind * GROUPS, GROUPS)

        def add_side(c, total):
            return total + lax.dot_general(
                rows[c, part], rows[c, BLOCK : 2 * BLOCK], along_rows, preferred_element_type=f32
            )

        scores[part, BLOCK : 2 * BLOCK] = lax.fori_loop(
            0, SUB, add_side, jnp.zeros((GROUPS, BLOCK), f32), unroll=UNROLL
        )
        apart = (iota((GROUPS, BLOCK), 0) + kind * GROUPS != iota((GROUPS, BLOCK), 1)).astype(f32)
        mask = jnp.concatenate([lives[0][0:1, :] * apart, side_mask], axis=1)
        raw = jnp.exp(score_scale * scores[part, :]) * mask
        weights[...] = raw.astype(bf16)
        denom = self_weight + jnp.sum(raw, axis=1, keepdims=True)
        scale = jnp.broadcast_to(math.sqrt(WIDTH) / denom, (GROUPS, LANE))

        @pl.loop(0, SUB, unroll=UNROLL)
        def _(c):
            numer = self_weight * rows[c, part].astype(f32) + jnp.dot(
                weights[...], rows[c], preferred_element_type=f32
            )
            spread(wide, c, kind * GROUPS, GROUPS, numer * scale)

    def r_home(t, j):
        to = x_peer(j)
        return remote(
            out_r.at[t * XS + to], ret_r.at[mirror(t), x], rb_send, rb_recv.at[t // BATCH],
            at(z_peer(t), to),
        )

    def s_back(k, j):
        four, to = pl.ds(k * QUAD, QUAD), x_peer(j)
        return remote(out_s.at[four, to], cand.at[four, x], mb_send, mb_recv.at[k], at(z, to))

    def s_home(t):
        return remote(back_s.at[t], ret_s.at[mirror(t)], sb_send, sb_recv, at(z_peer(t), x))

    smooth(0)

    @pl.loop(0, BATCHES)
    def _(b):
        out_r[pl.ds(b * BATCH * XS, BATCH * XS)] = docs_of(wide, b * BATCH * XS, BATCH * XS)

        @pl.when(b < FIRST)
        def _():
            r_batch(b, lambda t, j: r_home(t, j).start())

    local(out_r.at[x], ret_r.at[0, x], rb_recv.at[0])

    smooth(1)

    @pl.loop(0, QUADS)
    def _(k):
        four = pl.ds(k * QUAD, QUAD)
        out_s[four] = docs_of(wide, GROUPS + k * 16, 16).reshape(QUAD, XS, SUB, LANE)
        for j in range(1, XS):
            s_back(k, j).start()
        local(out_s.at[four, x], cand.at[four, x], mb_recv.at[k])

    def choose(t):
        chosen = cand[t, XS - 1].astype(f32)
        for k in range(XS - 1):
            flag = choice[pl.ds(t * XS + k, 1), :]
            flag = jnp.broadcast_to(jnp.concatenate([flag, flag], axis=1), (SUB, LANE))
            chosen = jnp.where(flag > 0.5, cand[t, k].astype(f32), chosen)
        back_s[t] = chosen.astype(bf16)

    @pl.loop(0, QUADS)
    def _(k):
        settle(cand.at[pl.ds(k * QUAD, QUAD)], mb_recv.at[k])
        for i in range(QUAD):
            t = k * QUAD + i
            choose(t)
            if i == 0:
                @pl.when(t > 0)
                def _():
                    s_home(t).start()
            else:
                s_home(t).start()

    @pl.loop(FIRST, BATCHES)
    def _(b):
        r_batch(b, lambda t, j: r_home(t, j).start())

    local(back_s.at[0], ret_s.at[0], sb_recv)

    @pl.loop(0, BATCHES)
    def _(b):
        two = pl.ds(b * BATCH, BATCH)
        settle(ret_r.at[two], rb_recv.at[b])
        put_wide(wide, b * BATCH * XS, ret_r[two].reshape(BATCH * XS, SUB, LANE))

    settle(ret_s, sb_recv)
    put_wide(wide, GROUPS, ret_s[...])

    @pl.loop(0, SUB, unroll=UNROLL)
    def _(c):
        got = gather(wide, c, SENT).astype(bf16)
        out_ref[:, chunk(c)] = jnp.dot(unpick[...], got, preferred_element_type=f32).astype(bf16)

    settle(marks.at[pl.ds(0, XS - 1)], lab_send.at[0])
    settle(marks.at[pl.ds(0, GROUPS - XS)], lab_send.at[1])
    settle(send_r.at[pl.ds(0, GROUPS - 1)], r_send)
    settle(send_s.at[pl.ds(0, ZS - 1)], s_send)
    settle(send_r.at[pl.ds(0, GROUPS - ZS)], m_send)
    settle(own, yr_send)
    settle(own, ys_send)
    settle(out_r.at[pl.ds(0, GROUPS - 1)], rb_send)
    settle(out_r.at[pl.ds(0, GROUPS - ZS)], mb_send)
    settle(back_s.at[pl.ds(0, ZS - 1)], sb_send)


def compact(embeddings, dest, labels):
    vmem = pl.BlockSpec(memory_space=pltpu.VMEM)
    dma = pltpu.SemaphoreType.DMA
    return pl.pallas_call(
        compact_kernel,
        out_shape=(
            jax.ShapeDtypeStruct((COUNT, WIDTH), bf16),
            jax.ShapeDtypeStruct((1, 1), i32),
        ),
        in_specs=[pl.BlockSpec(memory_space=pl.ANY)] * 2 + [vmem],
        out_specs=(vmem, vmem),
        scratch_shapes=[
            pltpu.VMEM((256, 128), i32),
            pltpu.VMEM((COUNT, WIDTH), bf16),
            pltpu.VMEM((COUNT, WIDTH), bf16),
            pltpu.VMEM((2, BLOCK * SUB, 128), f32),
            pltpu.VMEM((GROUPS, SUB, LANE), bf16),
            pltpu.VMEM((ZS, SUB, LANE), bf16),
            pltpu.VMEM((ZS, SUB, LANE), bf16),
            pltpu.VMEM((2, ZS, XS, SUB, LANE), bf16),
            pltpu.VMEM((2, 2, ZS, XS, SUB, LANE), bf16),
            pltpu.VMEM((SUB, 2 * BLOCK, LANE), bf16),
            pltpu.VMEM((GROUPS, SUB, LANE), bf16),
            pltpu.VMEM((ZS, XS, SUB, LANE), bf16),
            pltpu.VMEM((ZS, SUB, LANE), bf16),
            pltpu.VMEM((ZS, XS, SUB, LANE), bf16),
            pltpu.VMEM((ZS, XS, SUB, LANE), bf16),
            pltpu.VMEM((ZS, SUB, LANE), bf16),
            pltpu.VMEM((1, 128), i32),
            pltpu.VMEM((GROUPS, 1, 128), i32),
            pltpu.VMEM((2, GROUPS, 256), f32),
            pltpu.VMEM((GROUPS, 128), i32),
            pltpu.VMEM((SENT, COUNT), bf16),
            pltpu.VMEM((COUNT, SENT), bf16),
            pltpu.VMEM((2, 8, 128), f32),
            pltpu.VMEM((3, 8, BLOCK), f32),
            pltpu.VMEM((GROUPS, 128), f32),
            pltpu.VMEM((GROUPS, 2 * BLOCK), bf16),
            pltpu.VMEM((BLOCK, 2 * BLOCK), f32),
            dma((2,)), dma((2,)), dma((2,)),
            dma(()), dma((BATCHES,)), dma(()), dma((QUADS,)), dma(()), dma((QUADS,)),
            dma(()), dma((BATCHES,)), dma(()), dma((QUADS,)),
            dma(()), dma((BATCHES,)), dma(()), dma((QUADS,)), dma(()), dma(()),
        ],
        compiler_params=pltpu.CompilerParams(
            collective_id=0, has_side_effects=True, vmem_limit_bytes=40 << 20
        ),
    )(embeddings, dest, labels)


def on_device(embeddings, dest, labels):
    out, ok = compact(embeddings, dest.reshape(GROUPS * PAIRS * COUNT // 128, 128), labels)
    return lax.cond(ok.reshape(()) == 1, lambda: out, lambda: padded(embeddings, dest, labels))


def solution(mesh):
    in_specs = (P(("group", "pair"), None), P(), P("group", None))
    out_specs = P(("group", "pair"), None)
    return jax.shard_map(
        on_device, mesh=mesh, in_specs=in_specs, out_specs=out_specs, check_vma=False
    )
```

```python
import math

import jax
import jax.numpy as jnp
from jax import lax
from jax.experimental import pallas as pl
from jax.experimental.pallas import tpu as pltpu
from jax.sharding import PartitionSpec as P

score_scale = 64.0
self_weight = math.exp(4.0)
along_rows = (((1,), (1,)), ((), ()))
along_cols = (((0,), (0,)), ((), ()))


def shifted(block, axis, distance):
    devices = range(lax.axis_size(axis))
    route = [(i - distance, i) for i in devices if i - distance in devices]
    return lax.ppermute(block, axis, route)


def normalized(rows):
    values = rows.astype(jnp.float32)
    factor = lax.rsqrt(jnp.mean(values * values, axis=-1, keepdims=True) + 1e-05)
    return (values * factor * (1.0 / math.sqrt(values.shape[-1]))).astype(jnp.bfloat16)


def live_slots(routes, source_pair, owner, capacity):
    column = lax.dynamic_index_in_dim(routes, source_pair, axis=1, keepdims=False)
    counts = jnp.sum((column == owner).astype(jnp.int32), axis=1)
    return (
        (jnp.arange(capacity, dtype=jnp.int32)[None, :] < counts[:, None])
        .reshape(-1)
        .astype(jnp.float32)
    )


def pair_weights(left, right, mask):
    scores = lax.dot_general(left, right, along_rows, preferred_element_type=jnp.float32)
    return jnp.exp(score_scale * scores) * mask


def padded(embeddings, dest, labels):
    groups = lax.axis_size("group")
    pairs = lax.axis_size("pair")
    group_at = lax.axis_index("group")
    pair_at = lax.axis_index("pair")
    count = embeddings.shape[0]
    width = embeddings.shape[1]
    capacity = 2 * count // groups
    slots = groups * capacity
    routes = dest.reshape(groups, pairs, count)
    own_routes = lax.dynamic_index_in_dim(
        lax.dynamic_index_in_dim(routes, group_at, axis=0, keepdims=False),
        pair_at,
        axis=0,
        keepdims=False,
    )
    hits = (own_routes[:, None] == jnp.arange(groups, dtype=jnp.int32)[None, :]).astype(jnp.int32)
    ranks = jnp.sum(jnp.cumsum(hits, axis=0) * hits, axis=1) - 1
    slot = own_routes * capacity + ranks
    match = (slot[None, :] == jnp.arange(slots, dtype=jnp.int32)[:, None]).astype(jnp.int32)
    slot_doc = jnp.sum(match * jnp.arange(count, dtype=jnp.int32)[None, :], axis=1)
    filled = jnp.sum(match, axis=1)
    hat = normalized(embeddings)
    outgoing = jnp.where(filled[:, None] > 0, hat[slot_doc], jnp.zeros((), jnp.bfloat16))
    arrived = lax.all_to_all(
        outgoing.reshape(groups, capacity, width), "group", split_axis=0, concat_axis=0, tiled=True
    )
    block = arrived.reshape(slots, width)
    marks = labels[0]
    mine = marks[pair_at]
    live_mine = live_slots(routes, pair_at, group_at, capacity)
    next_at = jnp.minimum(pair_at + 1, pairs - 1)
    joined_next = jnp.logical_and(pair_at + 1 < pairs, marks[next_at] == mine).astype(jnp.float32)
    live_next = live_slots(routes, next_at, group_at, capacity)
    apart = (jnp.arange(slots)[:, None] != jnp.arange(slots)[None, :]).astype(jnp.float32)
    own_weights = pair_weights(block, block, live_mine[None, :] * apart)
    numer = self_weight * block.astype(jnp.float32) + jnp.dot(
        own_weights.astype(jnp.bfloat16), block, preferred_element_type=jnp.float32
    )
    denom = self_weight + jnp.sum(own_weights, axis=1)
    neighbour = shifted(block, "pair", -1)
    next_weights = pair_weights(
        block, neighbour, live_mine[:, None] * live_next[None, :] * joined_next
    )
    next_rounded = next_weights.astype(jnp.bfloat16)
    numer = numer + jnp.dot(next_rounded, neighbour, preferred_element_type=jnp.float32)
    denom = denom + jnp.sum(next_weights, axis=1)
    column_numer = lax.dot_general(
        next_rounded, block, along_cols, preferred_element_type=jnp.float32
    )
    column_denom = jnp.sum(next_weights, axis=0)
    came_numer, came_denom = (
        shifted(column_numer.astype(jnp.bfloat16), "pair", 1).astype(column_numer.dtype),
        shifted(column_denom.astype(jnp.bfloat16), "pair", 1).astype(column_denom.dtype),
    )
    numer = numer + came_numer
    denom = denom + came_denom
    block_out = (math.sqrt(width) * numer / denom[:, None]).astype(jnp.bfloat16)
    returned = lax.all_to_all(
        block_out.reshape(groups, capacity, width), "group", split_axis=0, concat_axis=0, tiled=True
    )
    return returned.reshape(slots, width)[slot]


ZS, XS, PAIRS, COUNT, WIDTH = 16, 4, 8, 64, 4096
GROUPS = ZS * XS
SUB, LANE = 16, 256
BLOCK = GROUPS * 2
SENT = GROUPS + ZS
BATCH = 2
BATCHES = ZS // BATCH
QUAD = 4
QUADS = ZS // QUAD
AHEAD = 5
UNROLL = 16
FIRST = 4
MESH = pl.DeviceIdType.MESH
f32, bf16, i32 = jnp.float32, jnp.bfloat16, jnp.int32


def distance_at(t):
    half = t // 2
    far = jnp.where(t % 2 == 0, 8 - half, 8 + half)
    return jnp.where(t == 0, 0, far)


def step_of(distance):
    near = jnp.where(distance < 8, 16 - 2 * distance, 2 * distance - 15)
    return jnp.where(distance == 0, 0, near)


def mirror(t):
    return jnp.where(t < 2, t, jnp.where(t % 2 == 0, t + 1, t - 1))


def iota(shape, axis):
    return lax.broadcasted_iota(i32, shape, axis)


def put_wide(wide, first, docs):
    n = docs.shape[0]
    flat = docs.astype(f32).reshape(n * SUB, LANE)
    for h in range(2):
        wide[h, pl.ds(pl.multiple_of(first * SUB, SUB), n * SUB), :] = flat[:, h * 128 : (h + 1) * 128]


def docs_of(wide, first, n):
    at = pl.ds(pl.multiple_of(first * SUB, SUB), n * SUB)
    flat = jnp.concatenate([wide[0, at, :], wide[1, at, :]], axis=1)
    return flat.astype(bf16).reshape(n, SUB, LANE)


def spread(wide, c, first, n, values):
    for h in range(2):
        wide[h, pl.ds(first * SUB + c, n, stride=SUB), :] = values[:, h * 128 : (h + 1) * 128]


def gather(wide, c, n):
    return jnp.concatenate([wide[h, pl.ds(c, n, stride=SUB), :] for h in range(2)], axis=1)


def chunk(c):
    return pl.ds(pl.multiple_of(c * LANE, LANE), LANE)


def compact_kernel(
    x_ref, dest_hbm, lab_ref, out_ref, ok_ref,
    dest_ref, xv, hat, wide, send_r, send_s, land_s, own, beside, rows, out_r, out_s, back_s, cand, ret_r, ret_s,
    mark, marks, counts, place, pick, unpick, sides, lives, choice, weights, scores,
    in_sem, lab_send, lab_recv,
    r_send, r_recv, s_send, s_recv, m_send, m_recv, yr_send, yr_recv, ys_send, ys_recv,
    rb_send, rb_recv, mb_send, mb_recv, sb_send, sb_recv,
):
    group = lax.axis_index("group")
    pair = lax.axis_index("pair")
    z, x = group // XS, group % XS

    def at(zz, xx):
        return (zz * XS + xx, pair)

    def z_peer(t):
        return lax.rem(z + distance_at(t), ZS)

    def x_peer(j):
        return lax.rem(x + j, XS)

    def pair_peer(side):
        return lax.rem(pair + jnp.where(side == 0, 1, PAIRS - 1), PAIRS)

    def remote(source, target, send, recv, device):
        return pltpu.make_async_remote_copy(
            source, target, send, recv, device_id=device, device_id_type=MESH
        )

    load_x = pltpu.make_async_copy(x_ref, xv, in_sem.at[0])
    load_dest = pltpu.make_async_copy(dest_hbm, dest_ref, in_sem.at[1])
    load_dest.start()
    load_x.start()
    barrier = pltpu.get_barrier_semaphore()

    @pl.loop(1, GROUPS)
    def _(d):
        pl.semaphore_signal(
            barrier, inc=1, device_id=(lax.rem(group + d, GROUPS), pair), device_id_type=MESH
        )

    for step in (1, PAIRS - 1):
        pl.semaphore_signal(
            barrier, inc=1, device_id=(group, lax.rem(pair + step, PAIRS)), device_id_type=MESH
        )

    load_dest.wait()
    turned = dest_ref[...].T
    for parity in range(2):
        part = turned[parity * COUNT : (parity + 1) * COUNT, :]
        unit = jnp.left_shift(jnp.ones_like(part), (part & 7) * 4)
        for k in range(GROUPS // 8):
            held = jnp.sum(jnp.where((part >> 3) == k, unit, 0), axis=0, keepdims=True)
            nibble = jnp.broadcast_to(held, (8, 256)) >> (iota((8, 256), 0) * 4)
            counts[parity, 8 * k : 8 * k + 8, :] = (nibble & 3).astype(f32)
    second = [(counts[parity] == 2.0).astype(f32) for parity in range(2)]
    both = (second[0] + second[1]).astype(bf16)
    need_col = jnp.sum(second[0] + second[1], axis=1, keepdims=True)
    need_row = lax.dot_general(
        jnp.ones((8, 256), bf16), both, along_rows, preferred_element_type=f32
    )[0:1, :]
    g_col, g_row = iota((GROUPS, GROUPS), 0), iota((GROUPS, GROUPS), 1)
    ahead = jnp.logical_or(
        need_row > need_col, jnp.logical_and(need_row == need_col, g_row < g_col)
    )
    standing = jnp.sum(ahead.astype(i32), axis=1, keepdims=True)
    position = (standing % ZS) * XS + standing // ZS
    place[...] = jnp.broadcast_to(position, (GROUPS, 128))

    cell = group * (PAIRS // 2) + pair // 2
    line = dest_ref[pl.ds(cell, 1), :]
    lane = iota((1, 128), 1)
    mine = lane // COUNT == pair % 2
    line = jnp.where(mine, line, -1)
    eye = iota((128, 128), 0) == iota((128, 128), 1)
    line_col = jnp.sum(jnp.where(eye, jnp.broadcast_to(line, (128, 128)), 0), axis=1, keepdims=True)
    earlier = jnp.logical_and(line_col == line, iota((128, 128), 0) < iota((128, 128), 1))
    rank = jnp.sum(earlier.astype(i32), axis=0, keepdims=True)
    spot = jnp.sum(
        jnp.where(iota((GROUPS, 128), 0) == line, place[...], 0), axis=0, keepdims=True
    )
    step = step_of((spot // XS - z + ZS) % ZS)
    slot = jnp.where(rank == 0, step * XS + spot % XS, GROUPS + step)
    slot = jnp.where(mine, slot, -1)
    fold = slot[:, :COUNT] + slot[:, COUNT:] + 1
    slot_col = jnp.sum(
        jnp.where(
            iota((COUNT, COUNT), 0) == iota((COUNT, COUNT), 1),
            jnp.broadcast_to(fold, (COUNT, COUNT)),
            0,
        ),
        axis=1,
        keepdims=True,
    )
    pick[...] = (iota((SENT, COUNT), 0) == fold).astype(f32).astype(bf16)
    unpick[...] = (iota((COUNT, SENT), 1) == slot_col).astype(f32).astype(bf16)
    mark[...] = jnp.zeros((1, 128), i32)
    mark[:, 0:PAIRS] = lab_ref[...]
    marks[pl.ds(group, 1), :, :] = mark[...].reshape(1, 1, 128)

    load_x.wait()

    @pl.loop(0, COUNT // 16)
    def _(i):
        r = pl.ds(pl.multiple_of(i * 16, 16), 16)
        values = xv[r, :].astype(f32)
        factor = lax.rsqrt(jnp.mean(values * values, axis=-1, keepdims=True) + 1e-05)
        hat[r, :] = (values * factor * (1.0 / math.sqrt(WIDTH))).astype(bf16)

    @pl.loop(0, SUB, unroll=UNROLL)
    def _(c):
        got = jnp.dot(pick[...], hat[:, chunk(c)], preferred_element_type=f32)
        spread(wide, c, 0, SENT, got)

    send_s[...] = docs_of(wide, GROUPS, ZS)

    def lab_x(j):
        here = marks.at[pl.ds(group, 1)]
        return remote(here, here, lab_send.at[0], lab_recv.at[0], at(z, x_peer(j)))

    def lab_z(t):
        here = marks.at[pl.ds(z * XS, XS)]
        return remote(here, here, lab_send.at[1], lab_recv.at[1], at(z_peer(t), x))

    def r_out(t, j):
        to = x_peer(j)
        return remote(
            send_r.at[t * XS + to], own.at[0, mirror(t), x], r_send, r_recv.at[t // BATCH],
            at(z_peer(t), to),
        )

    def s_out(t):
        return remote(send_s.at[t], land_s.at[mirror(t)], s_send, s_recv.at[t // QUAD], at(z_peer(t), x))

    def s_share(k, j):
        four = pl.ds(k * QUAD, QUAD)
        return remote(land_s.at[four], own.at[1, four, x], m_send, m_recv.at[k], at(z, x_peer(j)))

    def yr_out(b, side):
        two = pl.ds(b * BATCH, BATCH)
        return remote(
            own.at[0, two], beside.at[side, 0, two], yr_send, yr_recv.at[b],
            (group, pair_peer(side)),
        )

    def ys_out(k, side):
        four = pl.ds(k * QUAD, QUAD)
        return remote(
            own.at[1, four], beside.at[side, 1, four], ys_send, ys_recv.at[k],
            (group, pair_peer(side)),
        )

    def r_batch(b, act):
        for k in range(BATCH):
            t = b * BATCH + k
            for j in range(XS):
                if j == 0 and k == 0:
                    @pl.when(t > 0)
                    def _():
                        act(t, j)
                else:
                    act(t, j)

    def local(source, target, sem):
        pltpu.make_async_copy(source, target, sem).start()

    def settle(arrived, sem):
        pltpu.make_async_copy(arrived, arrived, sem).wait()

    pl.semaphore_wait(barrier, GROUPS - 1 + 2)

    for j in range(1, XS):
        lab_x(j).start()

    @pl.loop(1, ZS)
    def _(t):
        s_out(t).start()

    local(send_s.at[0], land_s.at[0], s_recv.at[0])

    @pl.loop(0, BATCHES)
    def _(b):
        send_r[pl.ds(b * BATCH * XS, BATCH * XS)] = docs_of(wide, b * BATCH * XS, BATCH * XS)

        @pl.when(b < AHEAD)
        def _():
            r_batch(b, lambda t, j: r_out(t, j).start())

    local(send_r.at[x], own.at[0, 0, x], r_recv.at[0])
    settle(marks.at[pl.ds(0, XS - 1)], lab_recv.at[0])

    @pl.loop(1, ZS)
    def _(t):
        lab_z(t).start()

    @pl.loop(0, QUADS)
    def _(k):
        four = pl.ds(k * QUAD, QUAD)
        settle(land_s.at[four], s_recv.at[k])
        for j in range(1, XS):
            s_share(k, j).start()
        local(land_s.at[four], own.at[1, four, x], m_recv.at[k])

    here = place[:, 0:1] == group
    held = [
        jnp.sum(jnp.where(here, counts[parity], 0.0), axis=0, keepdims=True) for parity in range(2)
    ]
    s_lane = iota((256, BLOCK), 1)
    s_source = lax.rem(z + distance_at((s_lane // XS) % ZS), ZS) * XS + s_lane % XS
    for n, shift in enumerate((0, PAIRS - 1, 1)):
        other = lax.rem(pair + shift, PAIRS)
        row = jnp.where(other % 2 == 0, held[0], held[1])
        chosen = (iota((256, BLOCK), 0) == s_source * (PAIRS // 2) + other // 2).astype(f32)
        filled = jnp.dot(
            jnp.broadcast_to(row, (8, 256)).astype(bf16), chosen.astype(bf16),
            preferred_element_type=f32,
        )
        lives[n] = (filled > (iota((8, BLOCK), 1) // GROUPS).astype(f32)).astype(f32)

    at_here = (place[:, 0:GROUPS] == z * XS + iota((GROUPS, GROUPS), 1) % XS).astype(f32)
    wanted = jnp.where(
        pair % 2 == 0, (counts[0] == 2.0).astype(f32), (counts[1] == 2.0).astype(f32)
    )
    owner_of = lax.dot_general(
        at_here.astype(bf16), wanted.astype(bf16), along_cols, preferred_element_type=f32
    )
    t_row = iota((GROUPS, 256), 0) // XS
    c_row = (lax.rem(z + distance_at(t_row), ZS) * XS + x) * (PAIRS // 2) + pair // 2
    choice[...] = jnp.broadcast_to(
        jnp.sum(jnp.where(iota((GROUPS, 256), 1) == c_row, owner_of, 0.0), axis=1, keepdims=True),
        (GROUPS, 128),
    )

    plane = (place[:, 0:ZS] // XS == iota((GROUPS, ZS), 1)).astype(f32).astype(bf16)
    most = jnp.zeros((1, 1), f32)
    for parity in range(2):
        load = lax.dot_general(
            plane, (counts[parity] == 2.0).astype(f32).astype(bf16), along_cols,
            preferred_element_type=f32,
        )
        most = jnp.maximum(most, jnp.max(jnp.max(load, axis=1, keepdims=True), axis=0, keepdims=True))
    ok_ref[...] = (most < 1.5).astype(i32)

    def read_labels():
        settle(marks.at[pl.ds(0, GROUPS - XS)], lab_recv.at[1])

        def add_marks(g, total):
            return total + jnp.where(place[pl.ds(g, 1), :] == group, marks[g], 0)

        label = lax.fori_loop(0, GROUPS, add_marks, jnp.zeros((1, 128), i32))

        def label_at(q):
            return jnp.sum(jnp.where(lane == q, label, 0), axis=1, keepdims=True)

        joined_prev = jnp.logical_and(label_at(pair - 1) == label_at(pair), pair > 0)
        joined_next = jnp.logical_and(label_at(pair + 1) == label_at(pair), pair < PAIRS - 1)
        sides[0] = jnp.broadcast_to(joined_prev.astype(f32), (8, 128))
        sides[1] = jnp.broadcast_to(joined_next.astype(f32), (8, 128))

    def to_rows(first):
        @pl.loop(0, SUB, unroll=UNROLL)
        def _(c):
            rows[c, pl.ds(pl.multiple_of(first, 16), 16), :] = gather(wide, c, 16).astype(bf16)

    def own_rows(kind, k):
        put_wide(wide, 0, own[kind, pl.ds(k * QUAD, QUAD)].reshape(16, SUB, LANE))
        to_rows(kind * GROUPS + k * 16)

    def beside_rows(kind, k):
        four = pl.ds(k * QUAD, QUAD)
        flag = sides[0][0:1, :]
        flag = jnp.broadcast_to(jnp.concatenate([flag, flag], axis=1), (16 * SUB, LANE))
        prev = beside[0, kind, four].reshape(16 * SUB, LANE).astype(f32)
        nxt = beside[1, kind, four].reshape(16 * SUB, LANE).astype(f32)
        put_wide(wide, 0, jnp.where(flag > 0.5, prev, nxt).reshape(16, SUB, LANE))
        to_rows(BLOCK + kind * GROUPS + k * 16)

    def beside_r(k):
        for i in range(2):
            two = pl.ds((2 * k + i) * BATCH, BATCH)
            settle(beside.at[:, 0, two], yr_recv.at[2 * k + i])
        beside_rows(0, k)

    @pl.loop(0, QUADS)
    def _(k):
        settle(own.at[1, pl.ds(k * QUAD, QUAD)], m_recv.at[k])
        for side in range(2):
            ys_out(k, side).start()

    @pl.loop(0, BATCHES)
    def _(b):
        settle(own.at[0, pl.ds(b * BATCH, BATCH)], r_recv.at[b])

        @pl.when(b + AHEAD < BATCHES)
        def _():
            r_batch(b + AHEAD, lambda t, j: r_out(t, j).start())

        for side in range(2):
            yr_out(b, side).start()

        @pl.when(b % 2 == 1)
        def _():
            own_rows(0, b // 2)
            own_rows(1, b // 2)

        pl.when(b == 3)(read_labels)

        @pl.when(b >= 4)
        def _():
            k = b - 4
            settle(beside.at[:, 1, pl.ds(k * QUAD, QUAD)], ys_recv.at[k])
            beside_rows(1, k)

            @pl.when(k >= 2)
            def _():
                beside_r(k - 2)

    def add_own(c, total):
        mine = rows[c, 0:BLOCK]
        return total + lax.dot_general(mine, mine, along_rows, preferred_element_type=f32)

    scores[:, 0:BLOCK] = lax.fori_loop(
        0, SUB, add_own, jnp.zeros((BLOCK, BLOCK), f32), unroll=UNROLL
    )

    @pl.loop(2, QUADS)
    def _(k):
        beside_r(k)

    prev_mask = lives[1][0:1, :] * sides[0][0:1, :]
    next_mask = lives[2][0:1, :] * sides[1][0:1, :]
    side_mask = jnp.broadcast_to(prev_mask + next_mask, (GROUPS, BLOCK))

    def smooth(kind):
        part = pl.ds(kind * GROUPS, GROUPS)

        def add_side(c, total):
            return total + lax.dot_general(
                rows[c, part], rows[c, BLOCK : 2 * BLOCK], along_rows, preferred_element_type=f32
            )

        scores[part, BLOCK : 2 * BLOCK] = lax.fori_loop(
            0, SUB, add_side, jnp.zeros((GROUPS, BLOCK), f32), unroll=UNROLL
        )
        apart = (iota((GROUPS, BLOCK), 0) + kind * GROUPS != iota((GROUPS, BLOCK), 1)).astype(f32)
        mask = jnp.concatenate([lives[0][0:1, :] * apart, side_mask], axis=1)
        raw = jnp.exp(score_scale * scores[part, :]) * mask
        weights[...] = raw.astype(bf16)
        denom = self_weight + jnp.sum(raw, axis=1, keepdims=True)
        scale = jnp.broadcast_to(math.sqrt(WIDTH) / denom, (GROUPS, LANE))

        @pl.loop(0, SUB, unroll=UNROLL)
        def _(c):
            numer = self_weight * rows[c, part].astype(f32) + jnp.dot(
                weights[...], rows[c], preferred_element_type=f32
            )
            spread(wide, c, kind * GROUPS, GROUPS, numer * scale)

    def r_home(t, j):
        to = x_peer(j)
        return remote(
            out_r.at[t * XS + to], ret_r.at[mirror(t), x], rb_send, rb_recv.at[t // BATCH],
            at(z_peer(t), to),
        )

    def s_back(k, j):
        four, to = pl.ds(k * QUAD, QUAD), x_peer(j)
        return remote(out_s.at[four, to], cand.at[four, x], mb_send, mb_recv.at[k], at(z, to))

    def s_home(t):
        return remote(back_s.at[t], ret_s.at[mirror(t)], sb_send, sb_recv, at(z_peer(t), x))

    smooth(0)

    @pl.loop(0, BATCHES)
    def _(b):
        out_r[pl.ds(b * BATCH * XS, BATCH * XS)] = docs_of(wide, b * BATCH * XS, BATCH * XS)

        @pl.when(b < FIRST)
        def _():
            r_batch(b, lambda t, j: r_home(t, j).start())

    local(out_r.at[x], ret_r.at[0, x], rb_recv.at[0])

    smooth(1)

    @pl.loop(0, QUADS)
    def _(k):
        four = pl.ds(k * QUAD, QUAD)
        out_s[four] = docs_of(wide, GROUPS + k * 16, 16).reshape(QUAD, XS, SUB, LANE)
        for j in range(1, XS):
            s_back(k, j).start()
        local(out_s.at[four, x], cand.at[four, x], mb_recv.at[k])

    def choose(t):
        chosen = cand[t, XS - 1].astype(f32)
        for k in range(XS - 1):
            flag = choice[pl.ds(t * XS + k, 1), :]
            flag = jnp.broadcast_to(jnp.concatenate([flag, flag], axis=1), (SUB, LANE))
            chosen = jnp.where(flag > 0.5, cand[t, k].astype(f32), chosen)
        back_s[t] = chosen.astype(bf16)

    @pl.loop(0, QUADS)
    def _(k):
        settle(cand.at[pl.ds(k * QUAD, QUAD)], mb_recv.at[k])
        for i in range(QUAD):
            t = k * QUAD + i
            choose(t)
            if i == 0:
                @pl.when(t > 0)
                def _():
                    s_home(t).start()
            else:
                s_home(t).start()

    @pl.loop(FIRST, BATCHES)
    def _(b):
        r_batch(b, lambda t, j: r_home(t, j).start())

    local(back_s.at[0], ret_s.at[0], sb_recv)

    @pl.loop(0, BATCHES)
    def _(b):
        two = pl.ds(b * BATCH, BATCH)
        settle(ret_r.at[two], rb_recv.at[b])
        put_wide(wide, b * BATCH * XS, ret_r[two].reshape(BATCH * XS, SUB, LANE))

    settle(ret_s, sb_recv)
    put_wide(wide, GROUPS, ret_s[...])

    @pl.loop(0, SUB, unroll=UNROLL)
    def _(c):
        got = gather(wide, c, SENT).astype(bf16)
        out_ref[:, chunk(c)] = jnp.dot(unpick[...], got, preferred_element_type=f32).astype(bf16)

    settle(marks.at[pl.ds(0, XS - 1)], lab_send.at[0])
    settle(marks.at[pl.ds(0, GROUPS - XS)], lab_send.at[1])
    settle(send_r.at[pl.ds(0, GROUPS - 1)], r_send)
    settle(send_s.at[pl.ds(0, ZS - 1)], s_send)
    settle(send_r.at[pl.ds(0, GROUPS - ZS)], m_send)
    settle(own, yr_send)
    settle(own, ys_send)
    settle(out_r.at[pl.ds(0, GROUPS - 1)], rb_send)
    settle(out_r.at[pl.ds(0, GROUPS - ZS)], mb_send)
    settle(back_s.at[pl.ds(0, ZS - 1)], sb_send)


def compact(embeddings, dest, labels):
    vmem = pl.BlockSpec(memory_space=pltpu.VMEM)
    dma = pltpu.SemaphoreType.DMA
    return pl.pallas_call(
        compact_kernel,
        out_shape=(
            jax.ShapeDtypeStruct((COUNT, WIDTH), bf16),
            jax.ShapeDtypeStruct((1, 1), i32),
        ),
        in_specs=[pl.BlockSpec(memory_space=pl.ANY)] * 2 + [vmem],
        out_specs=(vmem, vmem),
        scratch_shapes=[
            pltpu.VMEM((256, 128), i32),
            pltpu.VMEM((COUNT, WIDTH), bf16),
            pltpu.VMEM((COUNT, WIDTH), bf16),
            pltpu.VMEM((2, (BLOCK + 1) * SUB, 128), f32),
            pltpu.VMEM((GROUPS, SUB, LANE), bf16),
            pltpu.VMEM((ZS, SUB, LANE), bf16),
            pltpu.VMEM((ZS, SUB, LANE), bf16),
            pltpu.VMEM((2, ZS, XS, SUB, LANE), bf16),
            pltpu.VMEM((2, 2, ZS, XS, SUB, LANE), bf16),
            pltpu.VMEM((SUB, 2 * BLOCK, LANE), bf16),
            pltpu.VMEM((GROUPS, SUB, LANE), bf16),
            pltpu.VMEM((ZS, XS, SUB, LANE), bf16),
            pltpu.VMEM((ZS, SUB, LANE), bf16),
            pltpu.VMEM((ZS, XS, SUB, LANE), bf16),
            pltpu.VMEM((ZS, XS, SUB, LANE), bf16),
            pltpu.VMEM((ZS, SUB, LANE), bf16),
            pltpu.VMEM((1, 128), i32),
            pltpu.VMEM((GROUPS, 1, 128), i32),
            pltpu.VMEM((2, GROUPS, 256), f32),
            pltpu.VMEM((GROUPS, 128), i32),
            pltpu.VMEM((SENT, COUNT), bf16),
            pltpu.VMEM((COUNT, SENT), bf16),
            pltpu.VMEM((2, 8, 128), f32),
            pltpu.VMEM((3, 8, BLOCK), f32),
            pltpu.VMEM((GROUPS, 128), f32),
            pltpu.VMEM((GROUPS, 2 * BLOCK), bf16),
            pltpu.VMEM((BLOCK, 2 * BLOCK), f32),
            dma((2,)), dma((2,)), dma((2,)),
            dma(()), dma((BATCHES,)), dma(()), dma((QUADS,)), dma(()), dma((QUADS,)),
            dma(()), dma((BATCHES,)), dma(()), dma((QUADS,)),
            dma(()), dma((BATCHES,)), dma(()), dma((QUADS,)), dma(()), dma(()),
        ],
        compiler_params=pltpu.CompilerParams(
            collective_id=0, has_side_effects=True, vmem_limit_bytes=40 << 20
        ),
    )(embeddings, dest, labels)


def on_device(embeddings, dest, labels):
    out, ok = compact(embeddings, dest.reshape(GROUPS * PAIRS * COUNT // 128, 128), labels)
    return lax.cond(ok.reshape(()) == 1, lambda: out, lambda: padded(embeddings, dest, labels))


def solution(mesh):
    in_specs = (P(("group", "pair"), None), P(), P("group", None))
    out_specs = P(("group", "pair"), None)
    return jax.shard_map(
        on_device, mesh=mesh, in_specs=in_specs, out_specs=out_specs, check_vma=False
    )
```
